256 devices in a mesh: dp: 16 (over z_lo, y, core), fsdp: 16 (over x, z_hi).
Axes of the slice: x: 4, y: 4, z: 8 (z_hi: 4, z_lo: 2; z = z_hi * 2 + z_lo), core: 2. Of those that a mesh axis runs over, the one named last changes fastest.
Arguments:
- rows_owned: bfloat16 [16, 16, 256, 8192], P('dp', 'fsdp'), may hold values from -6 to 6
- target: int32 [16, 16, 256], P('dp', 'fsdp'), may hold values from 0 to 15, as said below
- offset: int32 [16, 16, 256], P('dp', 'fsdp'), may hold values from 0 to 255, as said below
- queries: bfloat16 [16, 16, 256, 4096], P('dp', 'fsdp'), may hold values from -6 to 6
- keys: bfloat16 [16, 16, 256, 512], P('dp', 'fsdp'), may hold values from -6 to 6
- cotangent: bfloat16 [16, 16, 256, 4096], P('dp', 'fsdp'), may hold values from -0.0234375 to 0.0234375
- segment: int32 [16, 16, 256], P('dp', 'fsdp'), may hold values from 0 to 15, as said below
- norm_gain: bfloat16 [8192], P('fsdp'), may hold values from 0.099609375 to 1.8984375
- value_weight: bfloat16 [8192, 512], P('fsdp'), may hold values from -0.0625 to 0.0625
Outputs:
- returned: bfloat16 [16, 16, 256, 4096], P('dp', 'fsdp')
- value_grad_sum: float32 [8192, 512], P('fsdp')
The draws below stay inside these ranges and needn't reach their ends.
Inputs may be any that keep to these rules, and one draw needn't show every extreme that they name: `target`: within one fsdp index, every owner device sends exactly one rollout, a run of consecutive rows, to every trainer device of its dp group, the rollouts in order of trainer index; at most 32 rows go from one owner device to one trainer device, and exactly 32 for some pair. Within one fsdp index the pairs (target, offset) of all owner rows are distinct, so that every packed row of every trainer device receives exactly one row; consecutive rows of a rollout keep consecutive offsets. `segment`: equal ids on a trainer device mark the rows of one rollout, which stand together; ids never fall along a device's rows; the id of a packed row is the dp index of the owner device that sent it.
All inputs are finite; a program needn't handle non-finite values.
Results may differ from the reference program's by a relative error of at most 0.025.
Values may be sent and summed in bfloat16 or wider, within the bound.
A program may use at most 128 MiB of HBM per device.

```python
import math
import jax
import jax.numpy as jnp
from jax import lax

D = 8192
HEAD_DIM = 128
HEADS_Q = 32
KV_HEADS = 4
TOK_DEV = 256
QW = 4096
KVW = 512
ALL_ROWS = 65536
N_DP = 16
N_FSDP = 16


def packing(key):
    key = jax.random.fold_in(key, 101)
    capacity = 2 * TOK_DEV // N_DP
    remainder = TOK_DEV - capacity
    others = N_DP - 1
    typical_length = remainder // others
    leftover = remainder % others
    spread = max(min((typical_length - 1) // 2, (capacity - typical_length - 1) // 2), 0)
    key_list = jax.random.split(key, 4)
    wiggle = jax.random.randint(key_list[0], (N_FSDP, others), -spread, spread + 1).astype(jnp.int32)
    lengths = typical_length + wiggle - jnp.roll(wiggle, -1, axis=1) + (jnp.arange(others) < leftover).astype(jnp.int32)[None, :]
    lengths = jnp.concatenate([lengths, jnp.full((N_FSDP, 1), capacity, jnp.int32)], axis=1)
    shuffle = jax.vmap(lambda sub_key: jax.random.permutation(sub_key, N_DP))
    arrangement = shuffle(jax.random.split(key_list[1], N_FSDP)).astype(jnp.int32)
    lengths = jnp.take_along_axis(lengths, arrangement, axis=1)
    trainer_shift = shuffle(jax.random.split(key_list[2], N_FSDP)).astype(jnp.int32)
    owner_shift = shuffle(jax.random.split(key_list[3], N_FSDP)).astype(jnp.int32)
    chosen_index = (trainer_shift[:, None, :] + owner_shift[:, :, None]) % N_DP
    pair_lengths = jnp.take_along_axis(jnp.broadcast_to(lengths[:, None, :], (N_FSDP, N_DP, N_DP)), chosen_index, axis=2)
    return pair_lengths


def layout(key):
    pair_lengths = packing(key)
    owner_end = jnp.cumsum(pair_lengths, axis=2)
    owner_begin = owner_end - pair_lengths
    trainer_end = jnp.cumsum(pair_lengths, axis=1)
    trainer_begin = trainer_end - pair_lengths
    rows_here = jnp.arange(TOK_DEV, dtype=jnp.int32)
    target_rows = jnp.sum((owner_end[:, :, :, None] <= rows_here).astype(jnp.int32), axis=2)
    within = rows_here[None, None, :] - jnp.take_along_axis(owner_begin, target_rows, axis=2)
    offset_rows = jnp.take_along_axis(trainer_begin, target_rows, axis=2) + within
    segment_rows = jnp.sum((trainer_end[:, :, :, None] <= rows_here).astype(jnp.int32), axis=1)
    return (target_rows.transpose(1, 0, 2), offset_rows.transpose(1, 0, 2), segment_rows.transpose(1, 0, 2))


def draw_target(key, part):
    target_rows = layout(key)[0]
    return target_rows


def draw_offset(key, part):
    offset_rows = layout(key)[1]
    return offset_rows


def draw_segment(key, part):
    segment_rows = layout(key)[2]
    return segment_rows


def draw_queries(key, part):
    own_key = jax.random.fold_in(key, 4)
    shape_full = (N_DP, N_FSDP, TOK_DEV, HEADS_Q * HEAD_DIM)
    noise = jnp.clip(jax.random.normal(own_key, shape_full, jnp.float32), -6.0, 6.0)
    return noise.astype(jnp.bfloat16)


def draw_keys(key, part):
    own_key = jax.random.fold_in(key, 5)
    shape_full = (N_DP, N_FSDP, TOK_DEV, KV_HEADS * HEAD_DIM)
    noise = jnp.clip(jax.random.normal(own_key, shape_full, jnp.float32), -6.0, 6.0)
    return noise.astype(jnp.bfloat16)


def raised(result, key, source, target, blocks, factor):
    owner, partner = [(jnp.arange(result.shape[dim]) // (result.shape[dim] // blocks)).reshape([-1 if axis == dim else 1 for axis in range(result.ndim)]) for dim in (source, target)]
    chosen = jax.random.permutation(key, blocks)[partner]
    strong = (owner == chosen) | (owner == (partner + blocks // 2) % blocks)
    return jnp.where(strong, factor * result, result)


def block_levels(key, extent, cuts, least, largest):
    level, own = 1.0, jax.random.fold_in(key, 6)
    for dim, blocks in cuts:
        draws = jnp.exp(jax.random.uniform(jax.random.fold_in(own, dim), (blocks,), jnp.float32, least / len(cuts), largest / len(cuts)))
        level = level * jnp.repeat(draws, extent[dim] // blocks).reshape([-1 if axis == dim else 1 for axis in range(len(extent))])
    return level


def scatter_about(stream_key, dims, scale, reach, pieces=(), kind=jnp.bfloat16):
    factor_of = block_levels(stream_key, dims, pieces, -0.22, 0.18) if pieces else 1.0
    array = jax.random.normal(stream_key, dims, jnp.float32) * scale * factor_of
    return jnp.minimum(jnp.maximum(array, -reach), reach).astype(kind)


def noise_with(key, extent, deviation, reach, pieces, heavy, kind=jnp.bfloat16):
    array = deviation * jax.random.normal(key, extent, jnp.float32)
    if pieces:
        array = array * block_levels(key, extent, pieces, -0.22, 0.18)
    return jnp.clip(raised(array, jax.random.fold_in(key, 3), *heavy), -reach, reach).astype(kind)


def setup_inputs(seed: int = 0) -> dict:
    splits = jax.random.split(jax.random.key(seed), 10)
    return {
        "rows_owned": noise_with(splits[0], (N_DP, N_FSDP, TOK_DEV, D), 1.0, 6.0, ((0, 16), (1, 16)), (1, 3, 16, 2.0)),
        "target": draw_target(jax.random.fold_in(splits[9], 71), 0),
        "offset": draw_offset(jax.random.fold_in(splits[9], 71), 0),
        "queries": draw_queries(jax.random.fold_in(splits[9], 71), 0),
        "keys": draw_keys(jax.random.fold_in(splits[9], 71), 0),
        "cotangent": scatter_about(splits[5], (N_DP, N_FSDP, TOK_DEV, QW), (1.0 / ALL_ROWS ** 0.5), 0.0234375, ((0, 16), (1, 16))),
        "segment": draw_segment(jax.random.fold_in(splits[9], 71), 0),
        "norm_gain": jnp.clip(1.0 + 0.18 * jax.random.normal(splits[7], (D,), jnp.float32), 0.099609375, 1.8984375).astype(jnp.bfloat16),
        "value_weight": scatter_about(splits[8], (D, KVW), D ** -0.5, 0.0625, ((0, 16),)),
    }


epsilon = 1e-05

def normalize(rows, norm_gain):
    widened = rows.astype(jnp.float32)
    inverse = lax.rsqrt(lax.optimization_barrier(jnp.mean(widened * widened, axis=1, keepdims=True)) + epsilon)
    return (widened * inverse * norm_gain.astype(jnp.float32)[None, :]).astype(jnp.bfloat16)

def softmax_weights(queries, keys, segment):
    row_count = queries.shape[0]
    group_size = HEADS_Q // KV_HEADS
    query_heads = queries.astype(jnp.float32).reshape(row_count, KV_HEADS, group_size, HEAD_DIM)
    key_heads = keys.astype(jnp.float32).reshape(row_count, KV_HEADS, HEAD_DIM)
    scores = jnp.einsum('qgsd,kgd->gsqk', query_heads, key_heads) * (1.0 / math.sqrt(HEAD_DIM))
    position = jnp.arange(row_count, dtype=jnp.int32)
    allowed = (segment[:, None] == segment[None, :]) & (position[None, :] <= position[:, None])
    scores = jnp.where(allowed[None, None], scores, -1e+30)
    highest = lax.optimization_barrier(jnp.max(scores, axis=-1, keepdims=True))
    powers = jnp.exp(scores - highest)
    return (powers / lax.optimization_barrier(jnp.sum(powers, axis=-1, keepdims=True))).astype(jnp.bfloat16)

def trainer_pass(packed, queries, keys, cotangent, segment, norm_gain, value_weight):
    row_count = packed.shape[0]
    group_size = HEADS_Q // KV_HEADS
    normed = normalize(packed, norm_gain)
    values = jnp.dot(normed, value_weight, preferred_element_type=jnp.float32).astype(jnp.bfloat16)
    probabilities = softmax_weights(queries, keys, segment)
    weights_wide = probabilities.astype(jnp.float32)
    value_heads = values.astype(jnp.float32).reshape(row_count, KV_HEADS, HEAD_DIM)
    attended = jnp.einsum('gsqk,kgd->qgsd', weights_wide, value_heads).astype(jnp.bfloat16)
    attended = attended.reshape(row_count, HEADS_Q * HEAD_DIM)
    upstream = cotangent.astype(jnp.float32).reshape(row_count, KV_HEADS, group_size, HEAD_DIM)
    value_grad = jnp.einsum('gsqk,qgsd->kgd', weights_wide, upstream).astype(jnp.bfloat16)
    value_grad = value_grad.reshape(row_count, KV_HEADS * HEAD_DIM)
    return (attended, value_grad)

def flatten(tensor):
    return tensor.reshape((N_DP * N_FSDP,) + tensor.shape[2:])

def reference(rows_owned, target, offset, queries, keys, cotangent, segment, norm_gain, value_weight):
    column = jnp.broadcast_to(jnp.arange(N_FSDP, dtype=jnp.int32)[None, :, None], target.shape)
    owner_index = jnp.broadcast_to(jnp.arange(N_DP, dtype=jnp.int32)[:, None, None], target.shape)
    within = jnp.broadcast_to(jnp.arange(TOK_DEV, dtype=jnp.int32)[None, None, :], target.shape)
    source_owner = jnp.zeros_like(target).at[target, column, offset].set(owner_index)
    source_row = jnp.zeros_like(target).at[target, column, offset].set(within)

    def advance(carry, inputs_now):
        device_index, owners, owner_rows, query_rows, key_rows, cotangent_rows, segment_rows = inputs_now
        fsdp_index = device_index % N_FSDP
        packed = rows_owned[owners, fsdp_index, owner_rows]
        attended, value_grad = trainer_pass(packed, query_rows, key_rows, cotangent_rows, segment_rows, norm_gain, value_weight)
        return (carry, (attended, value_grad))
    device_ids = jnp.arange(N_DP * N_FSDP, dtype=jnp.int32)
    _, (attended, packed_grad) = lax.scan(advance, jnp.zeros((), jnp.float32), (device_ids, flatten(source_owner), flatten(source_row), flatten(queries), flatten(keys), flatten(cotangent), flatten(segment)))
    attended = attended.reshape(N_DP, N_FSDP, TOK_DEV, HEADS_Q * HEAD_DIM)
    packed_grad = packed_grad.reshape(N_DP, N_FSDP, TOK_DEV, KV_HEADS * HEAD_DIM)
    returned = attended[target, column, offset]
    owner_grad = packed_grad[target, column, offset]

    def accumulate(gradient_sum, inputs_now):
        owner_rows, grad_rows = inputs_now
        normed = normalize(owner_rows, norm_gain)
        partial_value = lax.dot_general(normed, grad_rows, (((0,), (0,)), ((), ())), preferred_element_type=jnp.float32)
        partial_value = lax.optimization_barrier(partial_value.astype(jnp.bfloat16)).astype(jnp.float32)
        return (gradient_sum + partial_value, None)
    gradient_sum, _ = lax.scan(accumulate, jnp.zeros((D, KV_HEADS * HEAD_DIM), jnp.float32), (flatten(rows_owned), flatten(owner_grad)))
    return (returned, gradient_sum)
```

```python
import math

import jax
import jax.numpy as jnp
from jax import lax
from jax.experimental import pallas as pl
from jax.experimental.pallas import tpu as pltpu
from jax.sharding import PartitionSpec as P

HEAD_DIM = 128
HEADS_Q = 32
KV_HEADS = 4
GROUP = HEADS_Q // KV_HEADS
TOK = 256
D = 8192
QW = HEADS_Q * HEAD_DIM
KVW = KV_HEADS * HEAD_DIM
N_DP = 16
N_FSDP = 16
CAP = 32
SLOTS = N_DP * CAP
DSH = D // N_FSDP
DC = DSH // 2
DH = D // 2
EPS = 1e-05
ROWS_X = 128
ROWS_Y = (DC - ROWS_X) // 4
F32 = jnp.float32
BF16 = jnp.bfloat16
MESH = pl.DeviceIdType.MESH
NT = (((1,), (1,)), ((), ()))
TN = (((0,), (0,)), ((), ()))


def dot(a, b):
    return jnp.dot(a, b, preferred_element_type=F32)


def remote(src, dst, send_sem, recv_sem, device):
    return pltpu.make_async_remote_copy(
        src_ref=src, dst_ref=dst, send_sem=send_sem, recv_sem=recv_sem,
        device_id=device, device_id_type=MESH,
    )


def slot_matrices(ids):
    wide = jnp.broadcast_to(ids.astype(F32), (TOK, TOK))
    tall = wide.T
    begin = jnp.sum((tall < wide).astype(F32), axis=0, keepdims=True)
    place = lax.broadcasted_iota(jnp.int32, (1, TOK), 1).astype(F32)
    slot = ids.astype(F32) * CAP + place - begin
    slot_wide = jnp.broadcast_to(slot, (SLOTS, TOK))
    onehot = slot_wide == lax.broadcasted_iota(jnp.int32, (SLOTS, TOK), 0).astype(F32)
    return onehot.astype(F32).astype(BF16)


def kernel(
    rows_ref, target_ref, q_ref, keys_ref, cot_ref, seg_ref, gain_ref, w_ref,
    out_ref, grad_ref,
    r_all, r_other, w_all, q_buf, c_buf, w_buf, qr, cr, kb, pt_s, pt_r, g_s, g_r, g_own,
    gt, a_r, b_r, a2_r, b2_r, a1, b1, s3, r3, fin, v_s, v_r, vb, att, st_ref,
    local_sem, row_s, row_r, wx_s, wx_r, wy_s, wy_r, wx2_s, wx2_r, wy2_s, wy2_r,
    g_ss, g_rs, p_ss, p_rs, go_s, go_r, v_ss, v_rs,
    a_ss, a_rs, b_ss, b_rs, a2_ss, a2_rs, b2_ss, b2_rs, z_ss, z_rs, f_ss, f_rs,
):
    p = lax.axis_index("dp")
    f = lax.axis_index("fsdp")
    zl, y, c = p // 8, (p // 2) % 4, p % 2
    x, zh = f // 4, f % 4
    z = zh * 2 + zl
    sgn = 2 * zl - 1

    def at_z(zz, yy, xx):
        zz = lax.rem(zz + 16, 8)
        return (((zz % 2) * 4 + yy) * 2 + c, xx * 4 + zz // 2)

    def at_x(d):
        return (p, ((x + d) % 4) * 4 + zh)

    def at_y(d):
        return ((zl * 4 + (y + d) % 4) * 2 + c, f)

    sibling = ((zl * 4 + y) * 2 + (1 - c), f)

    loads = [
        pltpu.make_async_copy(w_ref.at[pl.ds(c * DC, DC)], w_buf, local_sem.at[0]),
        pltpu.make_async_copy(q_ref, q_buf, local_sem.at[1]),
        pltpu.make_async_copy(cot_ref, c_buf, local_sem.at[2]),
    ]
    for cp in loads:
        cp.start()

    def row_load(i, half):
        col = pl.multiple_of(i * DSH + half * DC, 128)
        to = pl.multiple_of(i * DC, 128)
        return col, to

    def start_rows(i, _):
        col, to = row_load(i, 1 - c)
        pltpu.make_async_copy(
            rows_ref.at[:, pl.ds(col, DC)], r_other.at[:, pl.ds(to, DC)], local_sem.at[3]
        ).start()
        col, to = row_load(i, c)
        pltpu.make_async_copy(
            rows_ref.at[:, pl.ds(col, DC)], r_all.at[pl.ds(0, TOK), pl.ds(to, DC)], local_sem.at[4]
        ).start()
        return 0

    lax.fori_loop(0, N_FSDP, start_rows, 0)

    barrier = pltpu.get_barrier_semaphore()

    def greet(i, _):
        pl.semaphore_signal(barrier, inc=1, device_id=((p + i) % 16, f), device_id_type=MESH)
        pl.semaphore_signal(barrier, inc=1, device_id=(p, (f + i) % 16), device_id_type=MESH)
        return 0

    lax.fori_loop(1, 16, greet, 0)

    def greet_z(i, _):
        pl.semaphore_signal(
            barrier, inc=1,
            device_id=(((1 - zl) * 4 + y) * 2 + c, x * 4 + (zh + i) % 4), device_id_type=MESH,
        )
        return 0

    lax.fori_loop(1, 4, greet_z, 0)

    def greet_xz(i, _):
        dx, dz = 1 + i // 3, 1 + i % 3
        pl.semaphore_signal(
            barrier, inc=1,
            device_id=(((1 - zl) * 4 + y) * 2 + c, ((x + dx) % 4) * 4 + (zh + dz) % 4),
            device_id_type=MESH,
        )
        return 0

    lax.fori_loop(0, 9, greet_xz, 0)
    pl.semaphore_wait(barrier, 30 + 3 + 9)

    loads[0].wait()
    own_gain = gain_ref[:, pl.ds(pl.multiple_of(c * DC, 128), DC)]
    eye = lax.broadcasted_iota(jnp.int32, (DC, DC), 0) == lax.broadcasted_iota(jnp.int32, (DC, DC), 1)
    diagonal = jnp.where(eye, jnp.broadcast_to(own_gain.astype(F32), (DC, DC)), 0.0).astype(BF16)
    w_all[f] = dot(diagonal, w_buf[...]).astype(BF16)

    y_rows = pl.ds(pl.multiple_of(ROWS_X + y * ROWS_Y, 16), ROWS_Y)

    def wx_copy(k):
        part = w_all.at[f, pl.ds(0, ROWS_X)]
        return remote(part, part, wx_s.at[k - 1], wx_r.at[k - 1], at_z(z + sgn * k, y, x))

    def wy_copy(i):
        part = w_all.at[f, y_rows]
        return remote(part, part, wy_s.at[i], wy_r.at[i], at_z(z + sgn * (i % 4), y, (x + i // 4) % 4))

    for k in (3, 2, 1):
        wx_copy(k).start()

    def start_wy(i, _):
        wy_copy(i).start()
        return 0

    lax.fori_loop(1, 16, start_wy, 0)

    row_copy = remote(r_other, r_all.at[pl.ds(TOK, TOK)], row_s, row_r, sibling)
    pltpu.make_async_copy(r_other, r_other, local_sem.at[3]).wait()
    row_copy.start()

    onehot = slot_matrices(seg_ref[...])
    keys_pad = dot(onehot, keys_ref[...]).astype(BF16).reshape(N_DP, 2, 16, KVW)
    kb[...] = jnp.zeros_like(kb)
    for g in range(KV_HEADS):
        lanes = slice(g * 128, (g + 1) * 128)
        kb[:, :, g, :, lanes] = keys_pad[:, :, :, lanes]
    loads[1].wait()
    loads[2].wait()
    for g in range(KV_HEADS):
        wide = slice(g * 1024, (g + 1) * 1024)
        lanes = slice(g * 128, (g + 1) * 128)
        q_pad = dot(onehot, q_buf[:, wide]).astype(BF16).reshape(N_DP, 2, 16, 1024)
        c_pad = dot(onehot, c_buf[:, wide]).astype(BF16).reshape(N_DP, 2, 16, 1024)
        for s in range(GROUP):
            part = slice(s * 128, (s + 1) * 128)
            qr[:, :, s, :, lanes] = q_pad[:, :, :, part]
            cr[:, :, s, :, lanes] = c_pad[:, :, :, part]

    row_i = lax.broadcasted_iota(jnp.int32, (128, 256), 0)
    col_i = lax.broadcasted_iota(jnp.int32, (128, 256), 1)
    allowed = (row_i // 64) * 16 + row_i % 16 <= (col_i // 128) * 16 + col_i % 16

    def g_copy(o):
        return remote(g_s.at[o], g_r.at[p], g_ss.at[o], g_rs.at[p], (o, f))

    def p_copy(o):
        return remote(pt_s.at[o], pt_r.at[p], p_ss.at[o], p_rs.at[p], (o, f))

    def trainer(o):
        scores = lax.dot_general(
            kb[o].reshape(128, KVW), qr[o].reshape(256, KVW), NT, preferred_element_type=F32
        )
        scores = jnp.where(allowed, scores * (1.0 / math.sqrt(HEAD_DIM)), -1e30)
        scores = scores.reshape(2, 4, 16, 256)
        highest = jnp.max(jnp.max(scores, axis=0, keepdims=True), axis=2, keepdims=True)
        powers = jnp.exp(scores - highest)
        total = jnp.sum(jnp.sum(powers, axis=0, keepdims=True), axis=2, keepdims=True)
        prob = (powers / total).astype(BF16).reshape(128, 256)
        pt_s[o, 0:64] = prob[0:64, 0:128]
        pt_s[o, 64:192] = prob[:, 128:256]
        grad = dot(prob, cr[o].reshape(256, KVW)).astype(BF16)
        for kh in range(2):
            for g in range(KV_HEADS):
                lanes = slice(g * 128, (g + 1) * 128)
                g_s[o, kh * 16:(kh + 1) * 16, lanes] = grad[kh * 64 + g * 16:kh * 64 + (g + 1) * 16, lanes]

    def trainer_step(i, _):
        o = (p + i) % 16
        trainer(o)
        g_copy(o).start()
        return 0

    lax.fori_loop(1, 16, trainer_step, 0)
    trainer(p)
    g_r[p] = g_s[p]
    pt_r[p] = pt_s[p]

    def start_p(i, _):
        p_copy((p + i) % 16).start()
        return 0

    lax.fori_loop(1, 16, start_p, 0)

    def wx2_copy(d):
        part = w_all.at[pl.ds(x * 4, 4), pl.ds(0, ROWS_X)]
        return remote(part, part, wx2_s.at[d - 1], wx2_r.at[d - 1], at_x(d))

    def wy2_copy(d):
        part = w_all.at[:, y_rows]
        return remote(part, part, wy2_s.at[d - 1], wy2_r.at[d - 1], at_y(d))

    for k in (1, 2, 3):
        wx_copy(k).wait_recv()

    pltpu.make_async_copy(r_other, r_other, local_sem.at[4]).wait()

    def square(i, acc):
        col = pl.ds(pl.multiple_of(i * 512, 128), 512)
        own = r_all[0:TOK, col].astype(F32)
        oth = r_other[:, col].astype(F32)
        both = own * own + oth * oth
        return acc + both[:, 0:128] + both[:, 128:256] + both[:, 256:384] + both[:, 384:512]

    squares = lax.fori_loop(0, DH // 512, square, jnp.zeros((TOK, 128), F32))
    inverse = lax.rsqrt(jnp.sum(squares, axis=1, keepdims=True) * (1.0 / D) + EPS)
    owner_hot = slot_matrices(target_ref[...])
    st_ref[...] = owner_hot

    def wait_g(i, _):
        o = (p + i) % 16
        remote(g_s.at[o], g_r.at[o], g_ss.at[o], g_rs.at[o], (o, f)).wait_recv()
        return 0

    lax.fori_loop(1, 16, wait_g, 0)
    owner_grad = lax.dot_general(owner_hot, g_r[...].reshape(SLOTS, KVW), TN, preferred_element_type=F32)
    g_own[0:TOK] = (owner_grad * inverse).astype(BF16)
    go_copy = remote(g_own.at[pl.ds(0, TOK)], g_own.at[pl.ds(TOK, TOK)], go_s, go_r, sibling)
    go_copy.start()
    for d in (2, 1, 3):
        wx2_copy(d).start()
    row_copy.wait()
    go_copy.wait()

    def a_copy(d):
        part = gt.at[pl.ds(0, 256), pl.ds(pl.multiple_of(((x + d) % 4) * 1024, 128), 1024)]
        return remote(part, a_r.at[d - 1], a_ss.at[d - 1], a_rs.at[d - 1], at_x(d))

    def b_copy(d):
        part = gt.at[pl.ds(pl.multiple_of(256 + ((y + d) % 4) * 64, 16), 64)]
        return remote(part, b_r.at[d - 1], b_ss.at[d - 1], b_rs.at[d - 1], at_y(d))

    grad_rows = g_own[...]

    def partial(i, base):
        col = pl.ds(pl.multiple_of(base + i * 512, 128), 512)
        gt[:, col] = lax.dot_general(grad_rows, r_all[:, col], TN, preferred_element_type=F32).astype(BF16)
        return base

    for d in (2, 1, 3, 0):
        lax.fori_loop(0, 2, partial, ((x + d) % 4) * 1024)
        if d:
            a_copy(d).start()
    for d in (2, 1, 3):
        b_copy(d).start()

    def wait_wy(i, _):
        wy_copy(i).wait_recv()
        return 0

    lax.fori_loop(1, 16, wait_wy, 0)
    for d in (2, 1, 3):
        wy2_copy(d).start()

    for d in (1, 2, 3):
        a_copy(d).wait_recv()
    own_cols = pl.ds(pl.multiple_of(x * 1024, 128), 1024)
    a1[...] = (
        gt[0:256, own_cols].astype(F32) + a_r[0].astype(F32) + a_r[1].astype(F32) + a_r[2].astype(F32)
    ).astype(BF16)

    def a2_copy(d):
        part = a1.at[pl.ds(pl.multiple_of(((y + d) % 4) * 64, 16), 64)]
        return remote(part, a2_r.at[d - 1], a2_ss.at[d - 1], a2_rs.at[d - 1], at_y(d))

    for d in (2, 1, 3):
        a2_copy(d).start()
    for d in (1, 2, 3):
        b_copy(d).wait_recv()
    own_rows = pl.ds(pl.multiple_of(256 + y * 64, 16), 64)
    b1[...] = (
        gt[own_rows].astype(F32) + b_r[0].astype(F32) + b_r[1].astype(F32) + b_r[2].astype(F32)
    ).astype(BF16)

    def b2_copy(d):
        part = b1.at[:, pl.ds(pl.multiple_of(((x + d) % 4) * 1024, 128), 1024)]
        return remote(part, b2_r.at[d - 1], b2_ss.at[d - 1], b2_rs.at[d - 1], at_x(d))

    for d in (2, 1, 3):
        b2_copy(d).start()

    for d in (1, 2, 3):
        wx2_copy(d).wait_recv()
        wy2_copy(d).wait_recv()

    def project(i, acc):
        return acc + dot(r_all[:, pl.ds(pl.multiple_of(i * DC, 128), DC)], w_all[i])

    v_s[...] = lax.fori_loop(0, N_FSDP, project, jnp.zeros((2 * TOK, KVW), F32))
    v_copy = remote(v_s.at[pl.ds(TOK, TOK)], v_r, v_ss, v_rs, sibling)
    v_copy.start()

    for d in (1, 2, 3):
        a2_copy(d).wait_recv()
    own_a = pl.ds(pl.multiple_of(y * 64, 16), 64)
    s3[0] = (
        a1[own_a].astype(F32) + a2_r[0].astype(F32) + a2_r[1].astype(F32) + a2_r[2].astype(F32)
    ).astype(BF16)
    for d in (1, 2, 3):
        b2_copy(d).wait_recv()
    s3[1] = (
        b1[:, own_cols].astype(F32) + b2_r[0].astype(F32) + b2_r[1].astype(F32) + b2_r[2].astype(F32)
    ).astype(BF16)

    def z_part(zz):
        zz = lax.rem(zz, 8)
        return s3.at[
            :, pl.ds(pl.multiple_of((zz % 2) * 32, 16), 32), pl.ds(pl.multiple_of((zz // 2) * DC, 128), DC)
        ]

    def z_copy(k):
        return remote(z_part(z + k), r3.at[k - 1], z_ss.at[k - 1], z_rs.at[k - 1], at_z(z + k, y, x))

    for k in (4, 3, 5, 2, 6, 1, 7):
        z_copy(k).start()

    v_copy.wait()
    values = ((v_s[0:TOK] + v_r[...]) * inverse).astype(BF16)
    values_pad = dot(st_ref[...], values).astype(BF16).reshape(N_DP, 2, 16, KVW)
    vb[...] = jnp.zeros_like(vb)
    for g in range(KV_HEADS):
        lanes = slice(g * 128, (g + 1) * 128)
        vb[:, :, g, :, lanes] = values_pad[:, :, :, lanes]

    for k in range(1, 8):
        z_copy(k).wait_recv()
    total = z_part(z)[...].astype(F32)
    for k in range(7):
        total = total + r3[k].astype(F32)
    fin[p] = (total * own_gain.astype(F32).reshape(1, 1, DC)).astype(BF16)

    def f_copy(i):
        return remote(fin.at[p], fin.at[p], f_ss.at[i - 1], f_rs.at[i - 1], ((p + i) % 16, f))

    def start_f(i, _):
        f_copy(i).start()
        return 0

    lax.fori_loop(1, 16, start_f, 0)

    def wait_p(i, _):
        o = (p + i) % 16
        remote(pt_s.at[o], pt_r.at[o], p_ss.at[o], p_rs.at[o], (o, f)).wait_recv()
        return 0

    lax.fori_loop(1, 16, wait_p, 0)

    def attend(t, _):
        v_t = vb[t].reshape(128, KVW)
        low = lax.dot_general(pt_r[t, 0:64], v_t[0:64], TN, preferred_element_type=F32).astype(BF16)
        high = lax.dot_general(pt_r[t, 64:192], v_t, TN, preferred_element_type=F32).astype(BF16)
        for half, part in ((0, low), (1, high)):
            for s in range(GROUP):
                for g in range(KV_HEADS):
                    lane = g * 1024 + s * 128
                    att[t, half * 16:(half + 1) * 16, lane:lane + 128] = (
                        part[s * 16:(s + 1) * 16, g * 128:(g + 1) * 128]
                    )
        return 0

    lax.fori_loop(0, N_DP, attend, 0)

    def place(i, _):
        col = pl.ds(pl.multiple_of(i * 512, 128), 512)
        out_ref[:, col] = lax.dot_general(
            st_ref[...], att[:, :, col].reshape(SLOTS, 512), TN, preferred_element_type=F32
        ).astype(BF16)
        return 0

    lax.fori_loop(0, QW // 512, place, 0)

    def wait_f(i, _):
        f_copy(i).wait_recv()
        return 0

    lax.fori_loop(1, 16, wait_f, 0)
    for core in range(2):
        for portion in range(2):
            pieces = []
            for yy in range(4):
                for zz in range(2):
                    pieces.append(fin[(zz * 4 + yy) * 2 + core, portion].astype(F32))
            tall = jnp.concatenate(pieces, axis=0)
            grad_ref[core * DC:(core + 1) * DC, portion * 256:(portion + 1) * 256] = tall.T

    for k in (1, 2, 3):
        wx_copy(k).wait_send()
        wx2_copy(k).wait_send()
        wy2_copy(k).wait_send()
        a_copy(k).wait_send()
        b_copy(k).wait_send()
        a2_copy(k).wait_send()
        b2_copy(k).wait_send()
    for k in range(1, 8):
        z_copy(k).wait_send()

    def wait_sends(i, _):
        wy_copy(i).wait_send()
        g_copy((p + i) % 16).wait_send()
        p_copy((p + i) % 16).wait_send()
        f_copy(i).wait_send()
        return 0

    lax.fori_loop(1, 16, wait_sends, 0)


def on_device(rows_owned, target, offset, queries, keys, cotangent, segment, norm_gain, value_weight):
    dma = pltpu.SemaphoreType.DMA
    vmem = pltpu.VMEM
    scratch = [
        vmem((2 * TOK, DH), BF16),
        vmem((TOK, DH), BF16),
        vmem((N_FSDP, DC, KVW), BF16),
        vmem((TOK, QW), BF16),
        vmem((TOK, QW), BF16),
        vmem((DC, KVW), BF16),
        vmem((N_DP, 2, GROUP, 16, KVW), BF16),
        vmem((N_DP, 2, GROUP, 16, KVW), BF16),
        vmem((N_DP, 2, KV_HEADS, 16, KVW), BF16),
        vmem((N_DP, 192, 128), BF16),
        vmem((N_DP, 192, 128), BF16),
        vmem((N_DP, CAP, KVW), BF16),
        vmem((N_DP, CAP, KVW), BF16),
        vmem((2 * TOK, KVW), BF16),
        vmem((KVW, DH), BF16),
        vmem((3, 256, 1024), BF16),
        vmem((3, 64, DH), BF16),
        vmem((3, 64, 1024), BF16),
        vmem((3, 64, 1024), BF16),
        vmem((256, 1024), BF16),
        vmem((64, DH), BF16),
        vmem((2, 64, 1024), BF16),
        vmem((7, 2, 32, DC), BF16),
        vmem((N_DP, 2, 32, DC), BF16),
        vmem((2 * TOK, KVW), F32),
        vmem((TOK, KVW), F32),
        vmem((N_DP, 2, KV_HEADS, 16, KVW), BF16),
        vmem((N_DP, CAP, QW), BF16),
        vmem((SLOTS, TOK), BF16),
        dma((5,)),
        dma, dma,
        dma((3,)), dma((3,)), dma((16,)), dma((16,)),
        dma((3,)), dma((3,)), dma((3,)), dma((3,)),
        dma((16,)), dma((16,)), dma((16,)), dma((16,)),
        dma, dma, dma, dma,
        dma((3,)), dma((3,)), dma((3,)), dma((3,)),
        dma((3,)), dma((3,)), dma((3,)), dma((3,)),
        dma((7,)), dma((7,)), dma((15,)), dma((15,)),
    ]
    anywhere = pl.BlockSpec(memory_space=pl.ANY)
    inside = pl.BlockSpec(memory_space=pltpu.VMEM)
    returned, gradient = pl.pallas_call(
        kernel,
        out_shape=(
            jax.ShapeDtypeStruct((TOK, QW), BF16),
            jax.ShapeDtypeStruct((DSH, KVW), F32),
        ),
        in_specs=[anywhere, inside, anywhere, inside, anywhere, inside, inside, anywhere],
        out_specs=(inside, inside),
        scratch_shapes=scratch,
        compiler_params=pltpu.CompilerParams(
            collective_id=0, has_side_effects=True, vmem_limit_bytes=60 * 2**20
        ),
        cost_estimate=pl.CostEstimate(flops=8 * 10**9, bytes_accessed=16 * 2**20, transcendentals=10**6),
        name="value_path",
    )(
        rows_owned.reshape(TOK, D),
        target.reshape(1, TOK),
        queries.reshape(TOK, QW),
        keys.reshape(TOK, KVW),
        cotangent.reshape(TOK, QW),
        segment.reshape(1, TOK),
        norm_gain.reshape(1, DSH),
        value_weight,
    )
    return (returned.reshape(1, 1, TOK, QW), gradient)


def solution(mesh):
    placed = (
        P("dp", "fsdp", None, None),
        P("dp", "fsdp", None),
        P("dp", "fsdp", None),
        P("dp", "fsdp", None, None),
        P("dp", "fsdp", None, None),
        P("dp", "fsdp", None, None),
        P("dp", "fsdp", None),
        P("fsdp"),
        P("fsdp", None),
    )
    return jax.shard_map(
        on_device,
        mesh=mesh,
        in_specs=placed,
        out_specs=(P("dp", "fsdp", None, None), P("fsdp", None)),
        check_vma=False,
    )
```

```python
import math

import jax
import jax.numpy as jnp
from jax import lax
from jax.experimental import pallas as pl
from jax.experimental.pallas import tpu as pltpu
from jax.sharding import PartitionSpec as P

HEAD_DIM = 128
HEADS_Q = 32
KV_HEADS = 4
GROUP = HEADS_Q // KV_HEADS
TOK = 256
D = 8192
QW = HEADS_Q * HEAD_DIM
KVW = KV_HEADS * HEAD_DIM
N_DP = 16
N_FSDP = 16
CAP = 32
SLOTS = N_DP * CAP
DSH = D // N_FSDP
DC = DSH // 2
DH = D // 2
EPS = 1e-05
ROWS_X = 192
CHUNKS = 2
TRAIN = 3
ROWS_C = ROWS_X // CHUNKS
ROWS_Y = (DC - ROWS_X) // 4
F32 = jnp.float32
BF16 = jnp.bfloat16
MESH = pl.DeviceIdType.MESH
NT = (((1,), (1,)), ((), ()))
TN = (((0,), (0,)), ((), ()))


def dot(a, b):
    return jnp.dot(a, b, preferred_element_type=F32)


def remote(src, dst, send_sem, recv_sem, device):
    return pltpu.make_async_remote_copy(
        src_ref=src, dst_ref=dst, send_sem=send_sem, recv_sem=recv_sem,
        device_id=device, device_id_type=MESH,
    )


def slot_matrix(ids, tall_too=False):
    wide = jnp.broadcast_to(ids.astype(F32), (TOK, TOK))
    tall = wide.T
    begin = jnp.sum((tall < wide).astype(F32), axis=0, keepdims=True)
    place = lax.broadcasted_iota(jnp.int32, (1, TOK), 1).astype(F32)
    slot = ids.astype(F32) * CAP + place - begin
    slot_wide = jnp.broadcast_to(slot, (SLOTS, TOK))
    onehot = slot_wide == lax.broadcasted_iota(jnp.int32, (SLOTS, TOK), 0).astype(F32)
    onehot = onehot.astype(F32).astype(BF16)
    if not tall_too:
        return onehot
    slot_tall = jnp.broadcast_to(slot, (TOK, TOK)).T
    slot_tall = jnp.concatenate([slot_tall] * (SLOTS // TOK), axis=1)
    flipped = slot_tall == lax.broadcasted_iota(jnp.int32, (TOK, SLOTS), 1).astype(F32)
    return onehot, flipped.astype(F32).astype(BF16)


class RingGather:
    def __init__(self, part, me, device, send, recv, base=0):
        self.part, self.me, self.device = part, me, device
        self.send, self.recv, self.base = send, recv, base

    def copy(self, i):
        place, half, way = (
            (0, 0, 1), (0, 1, 1), (0, 1, -1), (0, 0, -1), (-1, 0, 1), (1, 1, -1)
        )[i]
        part = self.part((self.me + place) % 4, half)
        return remote(
            part, part, self.send.at[self.base + i], self.recv.at[self.base + i], self.device(way)
        )

    def start(self):
        for i in (0, 2, 1, 3):
            self.copy(i).start()

    def forward(self):
        for i in (0, 2):
            self.copy(i).wait_recv()
            self.copy(4 + i // 2).start()

    def finish(self):
        for i in (1, 3, 4, 5):
            self.copy(i).wait_recv()

    def wait_send(self):
        for i in range(6):
            self.copy(i).wait_send()


class RingReduce:
    def __init__(self, part, me, device, via, near, send, recv):
        self.part, self.me, self.device = part, me, device
        self.via, self.near, self.send, self.recv = via, near, send, recv

    def copy(self, i):
        place, half, way = ((2, 0, 1), (2, 1, -1), (1, 1, 1), (-1, 0, -1), (1, 0, 1), (-1, 1, -1))[i]
        to = self.via.at[half] if i < 2 else self.near.at[0 if way == 1 else 1, half]
        return remote(
            self.part((self.me + place) % 4, half), to, self.send.at[i], self.recv.at[i], self.device(way)
        )

    def forward(self):
        for half, place in ((0, 1), (1, -1)):
            self.copy(half).wait_recv()
            part = self.part((self.me + place) % 4, half)
            part[...] = (part[...].astype(F32) + self.via[half].astype(F32)).astype(BF16)
            self.copy(4 + half).start()

    def finish(self):
        for i in range(2, 6):
            self.copy(i).wait_recv()

    def total(self, half):
        own = self.part(self.me, half)[...].astype(F32)
        return own + self.near[0, half].astype(F32) + self.near[1, half].astype(F32)

    def wait_send(self):
        for i in range(6):
            self.copy(i).wait_send()


def kernel(
    rows_ref, target_ref, q_ref, keys_ref, cot_ref, seg_ref, gain_ref, w_ref,
    out_ref, grad_ref,
    r_all, r_other, w_all, q_buf, c_buf, w_buf, qr, cr, kb, pt_s, pt_r, g_s, g_r, g_own,
    gt, a_via, a_near, b_via, b_near, a2_r, b2_r, a1, b1, s3, r3, fin, v_s, v_r, vb, att, st_ref,
    ft_ref, gw,
    local_sem, row_s, row_r, wx_s, wx_r, wy_s, wy_r, wx2_s, wx2_r, wy2_s, wy2_r,
    g_ss, g_rs, p_ss, p_rs, go_s, go_r, v_ss, v_rs,
    a_ss, a_rs, b_ss, b_rs, a2_ss, a2_rs, b2_ss, b2_rs, z_ss, z_rs, f_ss, f_rs,
):
    p = lax.axis_index("dp")
    f = lax.axis_index("fsdp")
    zl, y, c = p // 8, (p // 2) % 4, p % 2
    x, zh = f // 4, f % 4
    z = zh * 2 + zl
    sgn = 2 * zl - 1

    def at_z(zz, yy, xx):
        zz = lax.rem(zz + 16, 8)
        return (((zz % 2) * 4 + yy) * 2 + c, xx * 4 + zz // 2)

    def at_x(d):
        return (p, ((x + d) % 4) * 4 + zh)

    def at_y(d):
        return ((zl * 4 + (y + d) % 4) * 2 + c, f)

    sibling = ((zl * 4 + y) * 2 + (1 - c), f)

    loads = [
        pltpu.make_async_copy(w_ref.at[pl.ds(c * DC, DC)], w_buf, local_sem.at[0]),
        pltpu.make_async_copy(q_ref, q_buf, local_sem.at[1]),
        pltpu.make_async_copy(cot_ref, c_buf, local_sem.at[2]),
    ]
    for cp in loads:
        cp.start()

    def row_load(i, half):
        col = pl.multiple_of(i * DSH + half * DC, 128)
        to = pl.multiple_of(i * DC, 128)
        return col, to

    def start_rows(i, _):
        col, to = row_load(i, 1 - c)
        pltpu.make_async_copy(
            rows_ref.at[:, pl.ds(col, DC)], r_other.at[:, pl.ds(to, DC)], local_sem.at[3]
        ).start()
        col, to = row_load(i, c)
        pltpu.make_async_copy(
            rows_ref.at[:, pl.ds(col, DC)], r_all.at[pl.ds(0, TOK), pl.ds(to, DC)], local_sem.at[4]
        ).start()
        return 0

    lax.fori_loop(0, N_FSDP, start_rows, 0)

    barrier = pltpu.get_barrier_semaphore()

    def greet(i, _):
        pl.semaphore_signal(barrier, inc=1, device_id=((p + i) % 16, f), device_id_type=MESH)
        pl.semaphore_signal(barrier, inc=1, device_id=(p, (f + i) % 16), device_id_type=MESH)
        return 0

    lax.fori_loop(1, 16, greet, 0)

    def greet_other(i, _):
        dx, dz = i // 3, 1 + i % 3
        pl.semaphore_signal(
            barrier, inc=1,
            device_id=(((1 - zl) * 4 + y) * 2 + c, ((x + dx) % 4) * 4 + (zh + dz) % 4),
            device_id_type=MESH,
        )
        return 0

    lax.fori_loop(0, 12, greet_other, 0)

    loads[0].wait()
    own_gain = gain_ref[:, pl.ds(pl.multiple_of(c * DC, 128), DC)]
    eye = lax.broadcasted_iota(jnp.int32, (DC, DC), 0) == lax.broadcasted_iota(jnp.int32, (DC, DC), 1)
    diagonal = jnp.where(eye, jnp.broadcast_to(own_gain.astype(F32), (DC, DC)), 0.0).astype(BF16)
    w_all[f] = dot(diagonal, w_buf[...]).astype(BF16)
    onehot = slot_matrix(seg_ref[...])
    pl.semaphore_wait(barrier, 30 + 12)

    y_rows = pl.ds(pl.multiple_of(ROWS_X + y * ROWS_Y, 16), ROWS_Y)

    def wx_copy(j, k):
        part = w_all.at[f, pl.ds(j * ROWS_C, ROWS_C)]
        i = j * 3 + k - 1
        return remote(part, part, wx_s.at[i], wx_r.at[i], at_z(z + sgn * k, y, x))

    def wy_copy(i):
        part = w_all.at[f, y_rows]
        return remote(part, part, wy_s.at[i], wy_r.at[i], at_z(z + sgn * (i % 4), y, (x + i // 4) % 4))

    for j in range(CHUNKS):
        for k in (3, 2, 1):
            wx_copy(j, k).start()

    def start_wy(i, _):
        wy_copy(i).start()
        return 0

    lax.fori_loop(1, 16, start_wy, 0)

    row_copy = remote(r_other, r_all.at[pl.ds(TOK, TOK)], row_s, row_r, sibling)
    pltpu.make_async_copy(r_other, r_other, local_sem.at[3]).wait()
    row_copy.start()

    keys_pad = dot(onehot, keys_ref[...]).astype(BF16).reshape(N_DP, 2, 16, KVW)
    kb[...] = jnp.zeros_like(kb)
    for g in range(KV_HEADS):
        lanes = slice(g * 128, (g + 1) * 128)
        kb[:, :, g, :, lanes] = keys_pad[:, :, :, lanes]
    loads[1].wait()
    loads[2].wait()
    for g in range(KV_HEADS):
        wide = slice(g * 1024, (g + 1) * 1024)
        lanes = slice(g * 128, (g + 1) * 128)
        q_pad = dot(onehot, q_buf[:, wide]).astype(BF16).reshape(N_DP, 2, 16, 1024)
        c_pad = dot(onehot, c_buf[:, wide]).astype(BF16).reshape(N_DP, 2, 16, 1024)
        for s in range(GROUP):
            part = slice(s * 128, (s + 1) * 128)
            qr[:, :, s, :, lanes] = q_pad[:, :, :, part]
            cr[:, :, s, :, lanes] = c_pad[:, :, :, part]

    row_i = lax.broadcasted_iota(jnp.int32, (128, 256), 0)
    col_i = lax.broadcasted_iota(jnp.int32, (128, 256), 1)
    allowed = (row_i // 64) * 16 + row_i % 16 <= (col_i // 128) * 16 + col_i % 16

    def g_copy(o):
        return remote(g_s.at[o], g_r.at[p], g_ss.at[o], g_rs.at[p], (o, f))

    def p_copy(o):
        return remote(pt_s.at[o], pt_r.at[p], p_ss.at[o], p_rs.at[p], (o, f))

    def trainer(owners):
        scores = [
            lax.dot_general(
                kb[o].reshape(128, KVW), qr[o].reshape(256, KVW), NT, preferred_element_type=F32
            )
            for o in owners
        ]
        probs = []
        for o, score in zip(owners, scores):
            score = jnp.where(allowed, score * (1.0 / math.sqrt(HEAD_DIM)), -1e30)
            score = score.reshape(2, 4, 16, 256)
            highest = jnp.max(jnp.max(score, axis=0, keepdims=True), axis=2, keepdims=True)
            powers = jnp.exp(score - highest)
            total = jnp.sum(jnp.sum(powers, axis=0, keepdims=True), axis=2, keepdims=True)
            probs.append((powers / total).astype(BF16).reshape(128, 256))
        for o, prob in zip(owners, probs):
            grad = dot(prob, cr[o].reshape(256, KVW)).astype(BF16)
            for kh in range(2):
                for g in range(KV_HEADS):
                    lanes = slice(g * 128, (g + 1) * 128)
                    g_s[o, kh * 16:(kh + 1) * 16, lanes] = (
                        grad[kh * 64 + g * 16:kh * 64 + (g + 1) * 16, lanes]
                    )
            pt_s[o, 0:64] = prob[0:64, 0:128]
            pt_s[o, 64:192] = prob[:, 128:256]

    def x_part(j):
        def part(xx, half):
            return w_all.at[pl.ds(xx * 4, 4), pl.ds(j * ROWS_C + half * (ROWS_C // 2), ROWS_C // 2)]

        return part

    wx2 = [RingGather(x_part(j), x, at_x, wx2_s, wx2_r, 6 * j) for j in range(CHUNKS)]

    def y_part(yy, half):
        rows = pl.ds(pl.multiple_of(ROWS_X + yy * ROWS_Y, 16), ROWS_Y)
        return w_all.at[pl.ds(half * 8, 8), rows]

    wy2 = RingGather(y_part, y, at_y, wy2_s, wy2_r)

    def trainer_step(i, _):
        owners = [(p + 1 + i * TRAIN + j) % 16 for j in range(TRAIN)]
        trainer(owners)
        for o in owners:
            g_copy(o).start()

        @pl.when(i == 1)
        def _():
            for k in (1, 2, 3):
                wx_copy(0, k).wait_recv()
            wx2[0].start()

        return 0

    lax.fori_loop(0, 15 // TRAIN, trainer_step, 0)
    trainer([p])
    g_r[p] = g_s[p]
    pt_r[p] = pt_s[p]

    def start_p(i, _):
        p_copy((p + i) % 16).start()
        return 0

    lax.fori_loop(1, 16, start_p, 0)
    for k in (1, 2, 3):
        wx_copy(1, k).wait_recv()
    wx2[0].forward()
    wx2[1].start()

    pltpu.make_async_copy(r_other, r_other, local_sem.at[4]).wait()

    def square(i, acc):
        col = pl.ds(pl.multiple_of(i * 512, 128), 512)
        own = r_all[0:TOK, col].astype(F32)
        oth = r_other[:, col].astype(F32)
        both = own * own + oth * oth
        return acc + both[:, 0:128] + both[:, 128:256] + both[:, 256:384] + both[:, 384:512]

    squares = lax.fori_loop(0, DH // 512, square, jnp.zeros((TOK, 128), F32))
    inverse = lax.rsqrt(jnp.sum(squares, axis=1, keepdims=True) * (1.0 / D) + EPS)
    owner_hot, owner_tall = slot_matrix(target_ref[...], True)
    st_ref[...] = owner_hot
    ft_ref[...] = owner_tall

    def wait_g(i, _):
        o = (p + i) % 16
        remote(g_s.at[o], g_r.at[o], g_ss.at[o], g_rs.at[o], (o, f)).wait_recv()
        return 0

    lax.fori_loop(1, 16, wait_g, 0)
    owner_grad = dot(owner_tall, g_r[...].reshape(SLOTS, KVW))
    g_own[0:TOK] = (owner_grad * inverse).astype(BF16)
    go_copy = remote(g_own.at[pl.ds(0, TOK)], g_own.at[pl.ds(TOK, TOK)], go_s, go_r, sibling)
    go_copy.start()
    row_copy.wait()

    def wait_wy(i, _):
        wy_copy(i).wait_recv()
        return 0

    lax.fori_loop(1, 16, wait_wy, 0)
    wy2.start()
    go_copy.wait()

    def a_part(xx, half):
        return gt.at[pl.ds(half * 128, 128), pl.ds(pl.multiple_of(xx * 1024, 128), 1024)]

    def b_part(yy, half):
        return gt.at[pl.ds(pl.multiple_of(256 + yy * 64 + half * 32, 16), 32)]

    ring_a = RingReduce(a_part, x, at_x, a_via, a_near, a_ss, a_rs)
    ring_b = RingReduce(b_part, y, at_y, b_via, b_near, b_ss, b_rs)
    gw[...] = g_own[...].T

    def partial(portion):
        def step(i, base):
            col = pl.ds(pl.multiple_of(base + i * 512, 128), 512)
            rows = slice(portion * 256, (portion + 1) * 256)
            gt[rows, col] = dot(gw[rows], r_all[:, col]).astype(BF16)
            return base

        return step

    def partial_a(d):
        lax.fori_loop(0, 2, partial(0), ((x + d) % 4) * 1024)

    partial_a(2)
    ring_a.copy(0).start()
    ring_a.copy(1).start()
    lax.fori_loop(0, 8, partial(1), 0)
    for i in (0, 1, 2, 3):
        ring_b.copy(i).start()
    partial_a(1)
    ring_a.copy(2).start()
    partial_a(3)
    ring_a.copy(3).start()
    partial_a(0)

    wx2[1].forward()
    wy2.forward()

    ring_a.forward()
    ring_b.forward()

    for ring in (wx2[0], wx2[1], wy2):
        ring.finish()
    for m in (1, 0):
        for n in range(2):
            cols = slice(n * 256, (n + 1) * 256)
            rows = slice(m * TOK, (m + 1) * TOK)
            v_s[rows, cols] = dot(r_all[rows], w_all[:, :, cols].reshape(DH, 256))
        if m == 1:
            v_copy = remote(v_s.at[pl.ds(TOK, TOK)], v_r, v_ss, v_rs, sibling)
            v_copy.start()

    ring_a.finish()
    for half in range(2):
        a1[half * 128:(half + 1) * 128] = ring_a.total(half).astype(BF16)

    def a2_copy(d):
        part = a1.at[pl.ds(pl.multiple_of(((y + d) % 4) * 64, 16), 64)]
        return remote(part, a2_r.at[d - 1], a2_ss.at[d - 1], a2_rs.at[d - 1], at_y(d))

    for d in (2, 1, 3):
        a2_copy(d).start()
    ring_b.finish()
    for half in range(2):
        b1[half * 32:(half + 1) * 32] = ring_b.total(half).astype(BF16)

    def b2_copy(d):
        part = b1.at[:, pl.ds(pl.multiple_of(((x + d) % 4) * 1024, 128), 1024)]
        return remote(part, b2_r.at[d - 1], b2_ss.at[d - 1], b2_rs.at[d - 1], at_x(d))

    for d in (2, 1, 3):
        b2_copy(d).start()

    v_copy.wait()
    values = ((v_s[0:TOK] + v_r[...]) * inverse).astype(BF16)
    values_pad = dot(st_ref[...], values).astype(BF16).reshape(N_DP, 2, 16, KVW)
    vb[...] = jnp.zeros_like(vb)
    for g in range(KV_HEADS):
        lanes = slice(g * 128, (g + 1) * 128)
        vb[:, :, g, :, lanes] = values_pad[:, :, :, lanes]

    def wait_p(i, _):
        o = (p + i) % 16
        remote(pt_s.at[o], pt_r.at[o], p_ss.at[o], p_rs.at[o], (o, f)).wait_recv()
        return 0

    lax.fori_loop(1, 16, wait_p, 0)

    def attend(i, _):
        for t in (2 * i, 2 * i + 1):
            v_t = vb[t].reshape(128, KVW)
            low = lax.dot_general(pt_r[t, 0:64], v_t[0:64], TN, preferred_element_type=F32).astype(BF16)
            high = lax.dot_general(pt_r[t, 64:192], v_t, TN, preferred_element_type=F32).astype(BF16)
            for half, part in ((0, low), (1, high)):
                for s in range(GROUP):
                    for g in range(KV_HEADS):
                        lane = g * 1024 + s * 128
                        att[t, half * 16:(half + 1) * 16, lane:lane + 128] = (
                            part[s * 16:(s + 1) * 16, g * 128:(g + 1) * 128]
                        )
        return 0

    lax.fori_loop(0, N_DP // 2, attend, 0)

    for d in (1, 2, 3):
        a2_copy(d).wait_recv()
    own_a = pl.ds(pl.multiple_of(y * 64, 16), 64)
    own_cols = pl.ds(pl.multiple_of(x * 1024, 128), 1024)
    s3[0] = (
        a1[own_a].astype(F32) + a2_r[0].astype(F32) + a2_r[1].astype(F32) + a2_r[2].astype(F32)
    ).astype(BF16)
    for d in (1, 2, 3):
        b2_copy(d).wait_recv()
    s3[1] = (
        b1[:, own_cols].astype(F32) + b2_r[0].astype(F32) + b2_r[1].astype(F32) + b2_r[2].astype(F32)
    ).astype(BF16)

    def z_part(zz):
        zz = lax.rem(zz, 8)
        return s3.at[
            :, pl.ds(pl.multiple_of((zz % 2) * 32, 16), 32), pl.ds(pl.multiple_of((zz // 2) * DC, 128), DC)
        ]

    def z_copy(k):
        return remote(z_part(z + k), r3.at[k - 1], z_ss.at[k - 1], z_rs.at[k - 1], at_z(z + k, y, x))

    for k in (4, 3, 5, 2, 6, 1, 7):
        z_copy(k).start()

    def place(i, _):
        col = pl.ds(pl.multiple_of(i * 512, 128), 512)
        out_ref[:, col] = dot(ft_ref[...], att[:, :, col].reshape(SLOTS, 512)).astype(BF16)
        return 0

    lax.fori_loop(0, QW // 512, place, 0)

    for k in range(1, 8):
        z_copy(k).wait_recv()
    total = z_part(z)[...].astype(F32)
    for k in range(7):
        total = total + r3[k].astype(F32)
    fin[p] = (total * own_gain.astype(F32).reshape(1, 1, DC)).astype(BF16)

    def f_copy(i):
        return remote(fin.at[p], fin.at[p], f_ss.at[i - 1], f_rs.at[i - 1], ((p + i) % 16, f))

    def start_f(i, _):
        f_copy(i).start()
        return 0

    lax.fori_loop(1, 16, start_f, 0)

    def wait_f(i, _):
        f_copy(i).wait_recv()
        return 0

    lax.fori_loop(1, 16, wait_f, 0)

    for core in range(2):
        for portion in range(2):
            pieces = []
            for yy in range(4):
                for zz in range(2):
                    pieces.append(fin[(zz * 4 + yy) * 2 + core, portion].astype(F32))
            tall = jnp.concatenate(pieces, axis=0)
            grad_ref[core * DC:(core + 1) * DC, portion * 256:(portion + 1) * 256] = tall.T

    for ring in (wx2[0], wx2[1], wy2, ring_a, ring_b):
        ring.wait_send()
    for k in (1, 2, 3):
        for j in range(CHUNKS):
            wx_copy(j, k).wait_send()
        a2_copy(k).wait_send()
        b2_copy(k).wait_send()
    for k in range(1, 8):
        z_copy(k).wait_send()

    def wait_sends(i, _):
        wy_copy(i).wait_send()
        g_copy((p + i) % 16).wait_send()
        p_copy((p + i) % 16).wait_send()
        f_copy(i).wait_send()
        return 0

    lax.fori_loop(1, 16, wait_sends, 0)


def on_device(rows_owned, target, offset, queries, keys, cotangent, segment, norm_gain, value_weight):
    dma = pltpu.SemaphoreType.DMA
    vmem = pltpu.VMEM
    scratch = [
        vmem((2 * TOK, DH), BF16),
        vmem((TOK, DH), BF16),
        vmem((N_FSDP, DC, KVW), BF16),
        vmem((TOK, QW), BF16),
        vmem((TOK, QW), BF16),
        vmem((DC, KVW), BF16),
        vmem((N_DP, 2, GROUP, 16, KVW), BF16),
        vmem((N_DP, 2, GROUP, 16, KVW), BF16),
        vmem((N_DP, 2, KV_HEADS, 16, KVW), BF16),
        vmem((N_DP, 192, 128), BF16),
        vmem((N_DP, 192, 128), BF16),
        vmem((N_DP, CAP, KVW), BF16),
        vmem((N_DP, CAP, KVW), BF16),
        vmem((2 * TOK, KVW), BF16),
        vmem((KVW, DH), BF16),
        vmem((2, 128, 1024), BF16),
        vmem((2, 2, 128, 1024), BF16),
        vmem((2, 32, DH), BF16),
        vmem((2, 2, 32, DH), BF16),
        vmem((3, 64, 1024), BF16),
        vmem((3, 64, 1024), BF16),
        vmem((256, 1024), BF16),
        vmem((64, DH), BF16),
        vmem((2, 64, 1024), BF16),
        vmem((7, 2, 32, DC), BF16),
        vmem((N_DP, 2, 32, DC), BF16),
        vmem((2 * TOK, KVW), F32),
        vmem((TOK, KVW), F32),
        vmem((N_DP, 2, KV_HEADS, 16, KVW), BF16),
        vmem((N_DP, CAP, QW), BF16),
        vmem((SLOTS, TOK), BF16),
        vmem((TOK, SLOTS), BF16),
        vmem((KVW, 2 * TOK), BF16),
        dma((5,)),
        dma, dma,
        dma((3 * CHUNKS,)), dma((3 * CHUNKS,)), dma((16,)), dma((16,)),
        dma((6 * CHUNKS,)), dma((6 * CHUNKS,)), dma((6,)), dma((6,)),
        dma((16,)), dma((16,)), dma((16,)), dma((16,)),
        dma, dma, dma, dma,
        dma((6,)), dma((6,)), dma((6,)), dma((6,)),
        dma((3,)), dma((3,)), dma((3,)), dma((3,)),
        dma((7,)), dma((7,)), dma((15,)), dma((15,)),
    ]
    anywhere = pl.BlockSpec(memory_space=pl.ANY)
    inside = pl.BlockSpec(memory_space=pltpu.VMEM)
    returned, gradient = pl.pallas_call(
        kernel,
        out_shape=(
            jax.ShapeDtypeStruct((TOK, QW), BF16),
            jax.ShapeDtypeStruct((DSH, KVW), F32),
        ),
        in_specs=[anywhere, inside, anywhere, inside, anywhere, inside, inside, anywhere],
        out_specs=(inside, inside),
        scratch_shapes=scratch,
        compiler_params=pltpu.CompilerParams(
            collective_id=0, has_side_effects=True, vmem_limit_bytes=60 * 2**20
        ),
        cost_estimate=pl.CostEstimate(flops=8 * 10**9, bytes_accessed=16 * 2**20, transcendentals=10**6),
        name="value_path",
    )(
        rows_owned.reshape(TOK, D),
        target.reshape(1, TOK),
        queries.reshape(TOK, QW),
        keys.reshape(TOK, KVW),
        cotangent.reshape(TOK, QW),
        segment.reshape(1, TOK),
        norm_gain.reshape(1, DSH),
        value_weight,
    )
    return (returned.reshape(1, 1, TOK, QW), gradient)


def solution(mesh):
    placed = (
        P("dp", "fsdp", None, None),
        P("dp", "fsdp", None),
        P("dp", "fsdp", None),
        P("dp", "fsdp", None, None),
        P("dp", "fsdp", None, None),
        P("dp", "fsdp", None, None),
        P("dp", "fsdp", None),
        P("fsdp"),
        P("fsdp", None),
    )
    return jax.shard_map(
        on_device,
        mesh=mesh,
        in_specs=placed,
        out_specs=(P("dp", "fsdp", None, None), P("fsdp", None)),
        check_vma=False,
    )
```

```python
import math

import jax
import jax.numpy as jnp
from jax import lax
from jax.experimental import pallas as pl
from jax.experimental.pallas import tpu as pltpu
from jax.sharding import PartitionSpec as P

HEAD_DIM = 128
HEADS_Q = 32
KV_HEADS = 4
GROUP = HEADS_Q // KV_HEADS
TOK = 256
D = 8192
QW = HEADS_Q * HEAD_DIM
KVW = KV_HEADS * HEAD_DIM
N_DP = 16
N_FSDP = 16
CAP = 32
SLOTS = N_DP * CAP
DSH = D // N_FSDP
DC = DSH // 2
DH = D // 2
EPS = 1e-05
ROWS_X = 96
CHUNKS = 1
TRAIN = 8
PARTS = 2
ROWS_C = ROWS_X // CHUNKS
ROWS_Y = 32
ROWS_Z = DC - ROWS_X - ROWS_Y
CHUNKS_Z = 2
ROWS_ZC = ROWS_Z // CHUNKS_Z
F32 = jnp.float32
BF16 = jnp.bfloat16
MESH = pl.DeviceIdType.MESH
NT = (((1,), (1,)), ((), ()))
TN = (((0,), (0,)), ((), ()))


def dot(a, b):
    return jnp.dot(a, b, preferred_element_type=F32)


def remote(src, dst, send_sem, recv_sem, device):
    return pltpu.make_async_remote_copy(
        src_ref=src, dst_ref=dst, send_sem=send_sem, recv_sem=recv_sem,
        device_id=device, device_id_type=MESH,
    )


def slot_matrix(ids, tall_too=False):
    wide = jnp.broadcast_to(ids.astype(F32), (TOK, TOK))
    tall = wide.T
    begin = jnp.sum((tall < wide).astype(F32), axis=0, keepdims=True)
    place = lax.broadcasted_iota(jnp.int32, (1, TOK), 1).astype(F32)
    slot = ids.astype(F32) * CAP + place - begin
    slot_wide = jnp.broadcast_to(slot, (SLOTS, TOK))
    onehot = slot_wide == lax.broadcasted_iota(jnp.int32, (SLOTS, TOK), 0).astype(F32)
    onehot = onehot.astype(F32).astype(BF16)
    if not tall_too:
        return onehot
    slot_tall = jnp.broadcast_to(slot, (TOK, TOK)).T
    slot_tall = jnp.concatenate([slot_tall] * (SLOTS // TOK), axis=1)
    flipped = slot_tall == lax.broadcasted_iota(jnp.int32, (TOK, SLOTS), 1).astype(F32)
    return onehot, flipped.astype(F32).astype(BF16)


class RingGather:
    def __init__(self, part, me, device, send, recv, base=0):
        self.part, self.me, self.device = part, me, device
        self.send, self.recv, self.base = send, recv, base

    def copy(self, i):
        place, half, way = (
            (0, 0, 1), (0, 1, 1), (0, 1, -1), (0, 0, -1), (-1, 0, 1), (1, 1, -1)
        )[i]
        part = self.part((self.me + place) % 4, half)
        return remote(
            part, part, self.send.at[self.base + i], self.recv.at[self.base + i], self.device(way)
        )

    def start(self):
        for i in (0, 2, 1, 3):
            self.copy(i).start()

    def forward(self):
        for i in (0, 2):
            self.copy(i).wait_recv()
            self.copy(4 + i // 2).start()

    def finish(self):
        for i in (1, 3, 4, 5):
            self.copy(i).wait_recv()

    def wait_send(self):
        for i in range(6):
            self.copy(i).wait_send()


class PairRingGather:
    def __init__(self, part, me, low, device, send, recv, base=0):
        self.part, self.me, self.low, self.device = part, me, low, device
        self.send, self.recv, self.base = send, recv, base

    def copy(self, i):
        out = 2 * self.low - 1
        place, half, way = (
            (0, None, out), (out, None, -out), (4 - out, 1 - self.low, out), (2, self.low, -out)
        )[i]
        part = self.part((self.me + place + 4) % 4, half)
        return remote(
            part, part, self.send.at[self.base + i], self.recv.at[self.base + i], self.device(way)
        )

    def step(self, i):
        if i:
            self.copy(i - 1).wait_recv()
        if i < 4:
            self.copy(i).start()

    def wait_send(self):
        for i in range(4):
            self.copy(i).wait_send()


class RingReduce:
    def __init__(self, part, me, device, via, near, send, recv, base=0):
        self.part, self.me, self.device = part, me, device
        self.via, self.near, self.send, self.recv, self.base = via, near, send, recv, base

    def copy(self, i):
        place, half, way = ((2, 0, 1), (2, 1, -1), (1, 1, 1), (-1, 0, -1), (1, 0, 1), (-1, 1, -1))[i]
        to = self.via.at[half] if i < 2 else self.near.at[0 if way == 1 else 1, half]
        return remote(
            self.part((self.me + place) % 4, half), to,
            self.send.at[self.base + i], self.recv.at[self.base + i], self.device(way),
        )

    def forward(self):
        for half, place in ((0, 1), (1, -1)):
            self.copy(half).wait_recv()
            part = self.part((self.me + place) % 4, half)
            part[...] = (part[...].astype(F32) + self.via[half].astype(F32)).astype(BF16)
            self.copy(4 + half).start()

    def finish(self):
        for i in range(2, 6):
            self.copy(i).wait_recv()

    def total(self, half):
        own = self.part(self.me, half)[...].astype(F32)
        return own + self.near[0, half].astype(F32) + self.near[1, half].astype(F32)

    def wait_send(self):
        for i in range(6):
            self.copy(i).wait_send()


def kernel(
    rows_ref, target_ref, q_ref, keys_ref, cot_ref, seg_ref, gain_ref, w_ref,
    out_ref, grad_ref,
    r_all, r_other, w_all, q_buf, c_buf, w_buf, qr, cr, kb, pt_s, pt_r, g_s, g_r, g_own,
    gt, a_via, a_near, b_via, b_near, a2_r, b2_r, a1, b1, s3, r3, fin, v_s, v_r, vb, out_buf, st_ref,
    ft_ref, gw,
    local_sem, row_s, row_r, wx_s, wx_r, wy_s, wy_r, wx2_s, wx2_r, wy2_s, wy2_r,
    wz_s, wz_r, wz2_s, wz2_r,
    g_ss, g_rs, p_ss, p_rs, go_s, go_r, v_ss, v_rs,
    a_ss, a_rs, b_ss, b_rs, a2_ss, a2_rs, b2_ss, b2_rs, z_ss, z_rs, f_ss, f_rs, fs_s, fs_r, out_sem,
):
    p = lax.axis_index("dp")
    f = lax.axis_index("fsdp")
    zl, y, c = p // 8, (p // 2) % 4, p % 2
    x, zh = f // 4, f % 4
    z = zh * 2 + zl
    sgn = 2 * zl - 1

    def at_z(zz, yy, xx):
        zz = lax.rem(zz + 16, 8)
        return (((zz % 2) * 4 + yy) * 2 + c, xx * 4 + zz // 2)

    def at_x(d):
        return (p, ((x + d) % 4) * 4 + zh)

    def at_y(d):
        return ((zl * 4 + (y + d) % 4) * 2 + c, f)

    sibling = ((zl * 4 + y) * 2 + (1 - c), f)

    loads = [
        pltpu.make_async_copy(w_ref.at[pl.ds(c * DC, DC)], w_buf, local_sem.at[0]),
        pltpu.make_async_copy(q_ref, q_buf, local_sem.at[1]),
        pltpu.make_async_copy(cot_ref, c_buf, local_sem.at[2]),
    ]
    for cp in loads:
        cp.start()

    def row_load(i, half):
        col = pl.multiple_of(i * DSH + half * DC, 128)
        to = pl.multiple_of(i * DC, 128)
        return col, to

    def start_rows(i, _):
        col, to = row_load(i, 1 - c)
        pltpu.make_async_copy(
            rows_ref.at[:, pl.ds(col, DC)], r_other.at[:, pl.ds(to, DC)], local_sem.at[3]
        ).start()
        col, to = row_load(i, c)
        pltpu.make_async_copy(
            rows_ref.at[:, pl.ds(col, DC)], r_all.at[pl.ds(0, TOK), pl.ds(to, DC)], local_sem.at[4]
        ).start()
        return 0

    lax.fori_loop(0, N_FSDP, start_rows, 0)

    barrier = pltpu.get_barrier_semaphore()

    def greet(i, _):
        pl.semaphore_signal(barrier, inc=1, device_id=((p + i) % 16, f), device_id_type=MESH)
        pl.semaphore_signal(barrier, inc=1, device_id=(p, (f + i) % 16), device_id_type=MESH)
        return 0

    lax.fori_loop(1, 16, greet, 0)

    def greet_other(i, _):
        dx, dz = i // 3, 1 + i % 3
        pl.semaphore_signal(
            barrier, inc=1,
            device_id=(((1 - zl) * 4 + y) * 2 + c, ((x + dx) % 4) * 4 + (zh + dz) % 4),
            device_id_type=MESH,
        )
        return 0

    lax.fori_loop(0, 12, greet_other, 0)

    loads[0].wait()
    own_gain = gain_ref[pl.ds(pl.multiple_of(c * DC, 128), DC)].reshape(1, DC)
    eye = lax.broadcasted_iota(jnp.int32, (DC, DC), 0) == lax.broadcasted_iota(jnp.int32, (DC, DC), 1)
    diagonal = jnp.where(eye, jnp.broadcast_to(own_gain.astype(F32), (DC, DC)), 0.0).astype(BF16)
    w_all[x, zh] = dot(diagonal, w_buf[...]).astype(BF16)
    onehot = slot_matrix(seg_ref[...])
    pl.semaphore_wait(barrier, 30 + 12)

    y_cols = pl.ds(pl.multiple_of(y * (KVW // 4), 128), KVW // 4)

    def wx_copy(j, k):
        part = w_all.at[x, zh, pl.ds(j * ROWS_C, ROWS_C)]
        i = j * 3 + k - 1
        return remote(part, part, wx_s.at[i], wx_r.at[i], at_z(z + sgn * k, y, x))

    def wy_copy(i):
        part = w_all.at[x, zh, pl.ds(ROWS_X, ROWS_Y), y_cols]
        return remote(part, part, wy_s.at[i], wy_r.at[i], at_z(z + sgn * (i % 4), y, (x + i // 4) % 4))

    def x_part(j):
        def part(xx, half):
            return w_all.at[xx, :, pl.ds(j * ROWS_C + half * (ROWS_C // 2), ROWS_C // 2)]

        return part

    wx2 = [RingGather(x_part(j), x, at_x, wx2_s, wx2_r, 6 * j) for j in range(CHUNKS)]

    def y_part(yy, half):
        cols = pl.ds(pl.multiple_of(yy * (KVW // 4), 128), KVW // 4)
        return w_all.at[pl.ds(half * 2, 2), :, pl.ds(ROWS_X, ROWS_Y), cols]

    wy2 = RingGather(y_part, y, at_y, wy2_s, wy2_r)

    first_z, rows_z = DC - ROWS_Z, ROWS_Z // 2

    def zx_part(xx, half):
        return w_all.at[xx, zh, pl.ds(first_z + half * rows_z, rows_z)]

    def z_ring_part(j):
        def part(zz, half):
            first = first_z + j * ROWS_ZC
            if half is None:
                return w_all.at[:, zz, pl.ds(first, ROWS_ZC)]
            first = first + half * (ROWS_ZC // 2)
            return w_all.at[:, zz, pl.ds(pl.multiple_of(first, 16), ROWS_ZC // 2)]

        return part

    wz = RingGather(zx_part, x, at_x, wz_s, wz_r)
    wz2 = [
        PairRingGather(z_ring_part(j), zh, zl, lambda way: at_z(z + way, y, x), wz2_s, wz2_r, 4 * j)
        for j in range(CHUNKS_Z)
    ]

    def step_wz2(i):
        for ring in wz2:
            ring.step(i)

    def start_wx(j):
        for k in (3, 2, 1):
            wx_copy(j, k).start()

    def start_wy(i, _):
        wy_copy(i).start()
        return 0

    wz.start()
    start_wx(0)

    row_copy = remote(r_other, r_all.at[pl.ds(TOK, TOK)], row_s, row_r, sibling)
    pltpu.make_async_copy(r_other, r_other, local_sem.at[3]).wait()
    row_copy.start()

    keys_pad = dot(onehot, keys_ref[...]).astype(BF16).reshape(N_DP, 2, 16, KVW)
    kb[...] = jnp.zeros_like(kb)
    for g in range(KV_HEADS):
        lanes = slice(g * 128, (g + 1) * 128)
        kb[:, :, g, :, lanes] = keys_pad[:, :, :, lanes]
    loads[1].wait()
    loads[2].wait()
    for g in range(KV_HEADS):
        wide = slice(g * 1024, (g + 1) * 1024)
        lanes = slice(g * 128, (g + 1) * 128)
        q_pad = dot(onehot, q_buf[:, wide]).astype(BF16).reshape(N_DP, 2, 16, 1024)
        c_pad = dot(onehot, c_buf[:, wide]).astype(BF16).reshape(N_DP, 2, 16, 1024)
        for s in range(GROUP):
            part = slice(s * 128, (s + 1) * 128)
            qr[:, :, s, :, lanes] = q_pad[:, :, :, part]
            cr[:, :, s, :, lanes] = c_pad[:, :, :, part]

    wz.forward()
    lax.fori_loop(1, 16, start_wy, 0)

    row_i = lax.broadcasted_iota(jnp.int32, (128, 256), 0)
    col_i = lax.broadcasted_iota(jnp.int32, (128, 256), 1)
    allowed = (row_i // 64) * 16 + row_i % 16 <= (col_i // 128) * 16 + col_i % 16

    def g_copy(o):
        return remote(g_s.at[o], g_r.at[p], g_ss.at[o], g_rs.at[p], (o, f))

    def p_copy(o):
        return remote(pt_s.at[o], pt_r.at[p], p_ss.at[o], p_rs.at[p], (o, f))

    def trainer(owners):
        scores = [
            lax.dot_general(
                kb[o].reshape(128, KVW), qr[o].reshape(256, KVW), NT, preferred_element_type=F32
            )
            for o in owners
        ]
        probs = []
        for o, score in zip(owners, scores):
            score = jnp.where(allowed, score * (1.0 / math.sqrt(HEAD_DIM)), -1e30)
            score = score.reshape(2, 4, 16, 256)
            highest = jnp.max(jnp.max(score, axis=0, keepdims=True), axis=2, keepdims=True)
            powers = jnp.exp(score - highest)
            total = jnp.sum(jnp.sum(powers, axis=0, keepdims=True), axis=2, keepdims=True)
            probs.append((powers / total).astype(BF16).reshape(128, 256))
        for o, prob in zip(owners, probs):
            grad = dot(prob, cr[o].reshape(256, KVW)).astype(BF16)
            for kh in range(2):
                for g in range(KV_HEADS):
                    lanes = slice(g * 128, (g + 1) * 128)
                    g_s[o, kh * 16:(kh + 1) * 16, lanes] = (
                        grad[kh * 64 + g * 16:kh * 64 + (g + 1) * 16, lanes]
                    )
            pt_s[o, 0:64] = prob[0:64, 0:128]
            pt_s[o, 64:192] = prob[:, 128:256]

    def trainer_step(i, _):
        owners = [(p + 1 + i * TRAIN + j) % 16 for j in range(TRAIN)]
        trainer(owners)
        for o in owners[:-1]:
            g_copy(o).start()

        @pl.when(i == 0)
        def _():
            g_copy(owners[-1]).start()

        return 0

    lax.fori_loop(0, 16 // TRAIN, trainer_step, 0)

    g_r[p] = g_s[p]
    pt_r[p] = pt_s[p]

    def wait_wx(j):
        for k in (1, 2, 3):
            wx_copy(j, k).wait_recv()

    wz.finish()
    step_wz2(0)
    wait_wx(0)
    wx2[0].start()

    pltpu.make_async_copy(r_other, r_other, local_sem.at[4]).wait()

    def square(i, acc):
        col = pl.ds(pl.multiple_of(i * 512, 128), 512)
        own = r_all[0:TOK, col].astype(F32)
        oth = r_other[:, col].astype(F32)
        both = own * own + oth * oth
        return acc + both[:, 0:128] + both[:, 128:256] + both[:, 256:384] + both[:, 384:512]

    squares = lax.fori_loop(0, DH // 512, square, jnp.zeros((TOK, 128), F32))
    inverse = lax.rsqrt(jnp.sum(squares, axis=1, keepdims=True) * (1.0 / D) + EPS)
    owner_hot, owner_tall = slot_matrix(target_ref[...], True)
    st_ref[...] = owner_hot
    ft_ref[...] = owner_tall

    def start_p(i, _):
        p_copy((p + i) % 16).start()
        return 0

    lax.fori_loop(1, 16, start_p, 0)

    def wait_g(i, _):
        o = (p + i) % 16
        remote(g_s.at[o], g_r.at[o], g_ss.at[o], g_rs.at[o], (o, f)).wait_recv()
        return 0

    lax.fori_loop(1, 16, wait_g, 0)

    owner_grad = dot(owner_tall, g_r[...].reshape(SLOTS, KVW))
    g_own[0:TOK] = (owner_grad * inverse).astype(BF16)
    go_copy = remote(g_own.at[pl.ds(0, TOK)], g_own.at[pl.ds(TOK, TOK)], go_s, go_r, sibling)
    go_copy.start()

    wx2[0].forward()

    def wait_wy(i, _):
        wy_copy(i).wait_recv()
        return 0

    lax.fori_loop(1, 16, wait_wy, 0)
    wy2.start()

    row_copy.wait()
    go_copy.wait()

    def a_part(q):
        def part(xx, half):
            return gt.at[
                pl.ds(q * 128 + half * 64, 64), pl.ds(pl.multiple_of(xx * 1024, 128), 1024)
            ]

        return part

    def b_part(q):
        def part(yy, half):
            return gt.at[pl.ds(pl.multiple_of(256 + yy * 64 + q * 32 + half * 16, 16), 16)]

        return part

    ring_a = [
        RingReduce(a_part(q), x, at_x, a_via.at[q], a_near.at[q], a_ss, a_rs, 6 * q) for q in range(PARTS)
    ]
    ring_b = [
        RingReduce(b_part(q), y, at_y, b_via.at[q], b_near.at[q], b_ss, b_rs, 6 * q) for q in range(PARTS)
    ]
    gw[...] = g_own[...].T

    def partial(d):
        col = pl.ds(pl.multiple_of(((x + d) % 4) * 1024, 128), 1024)
        gt[:, col] = dot(gw[...], r_all[:, col]).astype(BF16)

    partial(2)
    ring_a[0].copy(0).start()
    ring_a[0].copy(1).start()
    partial(1)
    ring_a[0].copy(2).start()
    partial(3)
    ring_a[0].copy(3).start()
    partial(0)
    for i in range(4):
        ring_b[0].copy(i).start()
    for i in range(4):
        ring_a[1].copy(i).start()
    for i in range(4):
        ring_b[1].copy(i).start()

    step_wz2(1)

    ring_a[0].forward()

    ring_b[0].forward()

    step_wz2(2)

    ring_a[1].forward()

    ring_b[1].forward()

    wy2.forward()

    def a2_copy(q, d):
        part = a1.at[q, pl.ds(pl.multiple_of(((y + d) % 4) * 32, 16), 32)]
        i = q * 3 + d - 1
        return remote(part, a2_r.at[q, d - 1], a2_ss.at[i], a2_rs.at[i], at_y(d))

    def b2_copy(q, d):
        part = b1.at[q, :, pl.ds(pl.multiple_of(((x + d) % 4) * 1024, 128), 1024)]
        i = q * 3 + d - 1
        return remote(part, b2_r.at[q, d - 1], b2_ss.at[i], b2_rs.at[i], at_x(d))

    def second_a(q):
        ring_a[q].finish()
        for half in range(2):
            a1[q, half * 64:(half + 1) * 64] = ring_a[q].total(half).astype(BF16)
        for d in (2, 1, 3):
            a2_copy(q, d).start()

    def second_b(q):
        ring_b[q].finish()
        for half in range(2):
            b1[q, half * 16:(half + 1) * 16] = ring_b[q].total(half).astype(BF16)
        for d in (2, 1, 3):
            b2_copy(q, d).start()

    second_a(0)
    second_b(0)

    step_wz2(3)

    second_a(1)

    second_b(1)

    for ring in wx2 + [wy2]:
        ring.finish()
    step_wz2(4)

    for n in range(2):
        cols = slice(n * 256, (n + 1) * 256)
        v_s[:, cols] = dot(r_all[...], w_all[:, :, :, cols].reshape(DH, 256))
    v_copy = remote(v_s.at[pl.ds(TOK, TOK)], v_r, v_ss, v_rs, sibling)
    v_copy.start()

    own_a = pl.ds(pl.multiple_of(y * 32, 16), 32)
    own_cols = pl.ds(pl.multiple_of(x * 1024, 128), 1024)

    def z_part(q, zz):
        zz = lax.rem(zz, 8)
        return s3.at[
            q, :, pl.ds(pl.multiple_of((zz % 2) * 16, 16), 16),
            pl.ds(pl.multiple_of((zz // 2) * DC, 128), DC),
        ]

    def z_copy(q, k):
        i = q * 7 + k - 1
        return remote(z_part(q, z + k), r3.at[q, k - 1], z_ss.at[i], z_rs.at[i], at_z(z + k, y, x))

    def third(q):
        for d in (1, 2, 3):
            a2_copy(q, d).wait_recv()
        total = a1[q, own_a].astype(F32)
        for d in range(3):
            total = total + a2_r[q, d].astype(F32)
        s3[q, 0] = total.astype(BF16)
        for d in (1, 2, 3):
            b2_copy(q, d).wait_recv()
        total = b1[q, :, own_cols].astype(F32)
        for d in range(3):
            total = total + b2_r[q, d].astype(F32)
        s3[q, 1] = total.astype(BF16)
        for k in (4, 3, 5, 2, 6, 1, 7):
            z_copy(q, k).start()

    third(0)

    third(1)

    v_copy.wait()
    values = ((v_s[0:TOK] + v_r[...]) * inverse).astype(BF16)
    values_pad = dot(st_ref[...], values).astype(BF16).reshape(N_DP, 2, 16, KVW)
    vb[...] = jnp.zeros_like(vb)
    for g in range(KV_HEADS):
        lanes = slice(g * 128, (g + 1) * 128)
        vb[:, :, g, :, lanes] = values_pad[:, :, :, lanes]

    def wait_p(i, _):
        o = (p + i) % 16
        remote(pt_s.at[o], pt_r.at[o], p_ss.at[o], p_rs.at[o], (o, f)).wait_recv()
        return 0

    lax.fori_loop(1, 16, wait_p, 0)

    def attend(i, _):
        for t in range(4):
            t = 4 * i + t
            v_t = vb[t].reshape(128, KVW)
            low = lax.dot_general(pt_r[t, 0:64], v_t[0:64], TN, preferred_element_type=F32).astype(BF16)
            high = lax.dot_general(pt_r[t, 64:192], v_t, TN, preferred_element_type=F32).astype(BF16)
            qr[t, 0] = low.reshape(GROUP, 16, KVW)
            qr[t, 1] = high.reshape(GROUP, 16, KVW)
        return 0

    lax.fori_loop(0, N_DP // 4, attend, 0)

    def f_copy(q, i):
        j = q * 7 + i - 1
        part = fin.at[q, c, p // 2]
        return remote(part, part, f_ss.at[j], f_rs.at[j], ((p // 2 + i) % 8 * 2 + c, f))

    def fs_copy(q):
        part = fin.at[q, c]
        return remote(part, part, fs_s.at[q], fs_r.at[q], sibling)

    def last(q):
        for k in range(1, 8):
            z_copy(q, k).wait_recv()
        total = z_part(q, z)[...].astype(F32)
        for k in range(7):
            total = total + r3[q, k].astype(F32)
        fin[q, c, p // 2] = (total * own_gain.astype(F32).reshape(1, 1, DC)).astype(BF16)

        def start_f(i, _):
            f_copy(q, i).start()
            return 0

        lax.fori_loop(1, 8, start_f, 0)

    last(0)

    last(1)

    out_copies = []
    for g in range(KV_HEADS):
        lanes = slice(g * 128, (g + 1) * 128)
        wide = slice(g * 1024, (g + 1) * 1024)
        heads = [qr[:, :, s, :, lanes].reshape(SLOTS, 128) for s in range(GROUP)]
        out_buf[:, wide] = dot(ft_ref[...], jnp.concatenate(heads, axis=1)).astype(BF16)
        out_copies.append(
            pltpu.make_async_copy(out_buf.at[:, wide], out_ref.at[:, wide], out_sem.at[g])
        )
        out_copies[-1].start()

    for q in range(PARTS):
        for i in range(1, 8):
            f_copy(q, i).wait_recv()
        fs_copy(q).start()
    for q in range(PARTS):
        fs_copy(q).wait_recv()

    for core in range(2):
        for portion in range(2):
            pieces = []
            for i in range(16):
                yy, q, zz = (i // 2 % 4, i // 8, i % 2) if portion == 0 else (i // 4, i // 2 % 2, i % 2)
                pieces.append(fin[q, core, zz * 4 + yy, portion].astype(F32))
            tall = jnp.concatenate(pieces, axis=0)
            grad_ref[core * DC:(core + 1) * DC, portion * 256:(portion + 1) * 256] = tall.T

    for cp in out_copies:
        cp.wait()
    for ring in wx2 + [wy2, wz] + wz2 + ring_a + ring_b:
        ring.wait_send()
    for k in (1, 2, 3):
        for j in range(CHUNKS):
            wx_copy(j, k).wait_send()
        for q in range(PARTS):
            a2_copy(q, k).wait_send()
            b2_copy(q, k).wait_send()
    for k in range(1, 8):
        for q in range(PARTS):
            z_copy(q, k).wait_send()
            f_copy(q, k).wait_send()
    for q in range(PARTS):
        fs_copy(q).wait_send()

    def wait_sends(i, _):
        wy_copy(i).wait_send()
        g_copy((p + i) % 16).wait_send()
        p_copy((p + i) % 16).wait_send()
        return 0

    lax.fori_loop(1, 16, wait_sends, 0)


def on_device(rows_owned, target, offset, queries, keys, cotangent, segment, norm_gain, value_weight):
    dma = pltpu.SemaphoreType.DMA
    vmem = pltpu.VMEM
    scratch = [
        vmem((2 * TOK, DH), BF16),
        vmem((TOK, DH), BF16),
        vmem((4, 4, DC, KVW), BF16),
        vmem((TOK, QW), BF16),
        vmem((TOK, QW), BF16),
        vmem((DC, KVW), BF16),
        vmem((N_DP, 2, GROUP, 16, KVW), BF16),
        vmem((N_DP, 2, GROUP, 16, KVW), BF16),
        vmem((N_DP, 2, KV_HEADS, 16, KVW), BF16),
        vmem((N_DP, 192, 128), BF16),
        vmem((N_DP, 192, 128), BF16),
        vmem((N_DP, CAP, KVW), BF16),
        vmem((N_DP, CAP, KVW), BF16),
        vmem((2 * TOK, KVW), BF16),
        vmem((KVW, DH), BF16),
        vmem((PARTS, 2, 64, 1024), BF16),
        vmem((PARTS, 2, 2, 64, 1024), BF16),
        vmem((PARTS, 2, 16, DH), BF16),
        vmem((PARTS, 2, 2, 16, DH), BF16),
        vmem((PARTS, 3, 32, 1024), BF16),
        vmem((PARTS, 3, 32, 1024), BF16),
        vmem((PARTS, 128, 1024), BF16),
        vmem((PARTS, 32, DH), BF16),
        vmem((PARTS, 2, 32, 1024), BF16),
        vmem((PARTS, 7, 2, 16, DC), BF16),
        vmem((PARTS, 2, 8, 2, 16, DC), BF16),
        vmem((2 * TOK, KVW), F32),
        vmem((TOK, KVW), F32),
        vmem((N_DP, 2, KV_HEADS, 16, KVW), BF16),
        vmem((TOK, QW), BF16),
        vmem((SLOTS, TOK), BF16),
        vmem((TOK, SLOTS), BF16),
        vmem((KVW, 2 * TOK), BF16),
        dma((5,)),
        dma, dma,
        dma((3 * CHUNKS,)), dma((3 * CHUNKS,)), dma((16,)), dma((16,)),
        dma((6 * CHUNKS,)), dma((6 * CHUNKS,)), dma((6,)), dma((6,)),
        dma((6,)), dma((6,)), dma((4 * CHUNKS_Z,)), dma((4 * CHUNKS_Z,)),
        dma((16,)), dma((16,)), dma((16,)), dma((16,)),
        dma, dma, dma, dma,
        dma((12,)), dma((12,)), dma((12,)), dma((12,)),
        dma((6,)), dma((6,)), dma((6,)), dma((6,)),
        dma((14,)), dma((14,)), dma((14,)), dma((14,)), dma((2,)), dma((2,)),
        dma((KV_HEADS,)),
    ]
    anywhere = pl.BlockSpec(memory_space=pl.ANY)
    inside = pl.BlockSpec(memory_space=pltpu.VMEM)
    returned, gradient = pl.pallas_call(
        kernel,
        out_shape=(
            jax.ShapeDtypeStruct((TOK, QW), BF16),
            jax.ShapeDtypeStruct((DSH, KVW), F32),
        ),
        in_specs=[anywhere, inside, anywhere, inside, anywhere, inside, inside, anywhere],
        out_specs=(anywhere, inside),
        scratch_shapes=scratch,
        compiler_params=pltpu.CompilerParams(
            collective_id=0, has_side_effects=True, vmem_limit_bytes=60 * 2**20
        ),
        cost_estimate=pl.CostEstimate(flops=8 * 10**9, bytes_accessed=16 * 2**20, transcendentals=10**6),
        name="value_path",
    )(
        rows_owned.reshape(TOK, D),
        target.reshape(1, TOK),
        queries.reshape(TOK, QW),
        keys.reshape(TOK, KVW),
        cotangent.reshape(TOK, QW),
        segment.reshape(1, TOK),
        norm_gain,
        value_weight,
    )
    return (returned.reshape(1, 1, TOK, QW), gradient)


def solution(mesh):
    placed = (
        P("dp", "fsdp", None, None),
        P("dp", "fsdp", None),
        P("dp", "fsdp", None),
        P("dp", "fsdp", None, None),
        P("dp", "fsdp", None, None),
        P("dp", "fsdp", None, None),
        P("dp", "fsdp", None),
        P("fsdp"),
        P("fsdp", None),
    )
    return jax.shard_map(
        on_device,
        mesh=mesh,
        in_specs=placed,
        out_specs=(P("dp", "fsdp", None, None), P("fsdp", None)),
        check_vma=False,
    )
```

```python
import math

import jax
import jax.numpy as jnp
from jax import lax
from jax.experimental import pallas as pl
from jax.experimental.pallas import tpu as pltpu
from jax.sharding import PartitionSpec as P

HEAD_DIM = 128
HEADS_Q = 32
KV_HEADS = 4
GROUP = HEADS_Q // KV_HEADS
TOK = 256
D = 8192
QW = HEADS_Q * HEAD_DIM
KVW = KV_HEADS * HEAD_DIM
N_DP = 16
N_FSDP = 16
CAP = 32
SLOTS = N_DP * CAP
DSH = D // N_FSDP
DC = DSH // 2
DH = D // 2
EPS = 1e-05
ROWS_X = 96
CHUNKS = ((0, 32), (32, 64))
ROWS_Z = DC - ROWS_X
CHUNKS_Z = ((0, 64), (64, 96))
FIRST_X = ROWS_Z
TRAIN = 8
PARTS = 2
PART_A = 256 // PARTS
PART_B = 64 // PARTS
HALF = DC // 2
F32 = jnp.float32
BF16 = jnp.bfloat16
MESH = pl.DeviceIdType.MESH
NT = (((1,), (1,)), ((), ()))
TN = (((0,), (0,)), ((), ()))


def dot(a, b):
    return jnp.dot(a, b, preferred_element_type=F32)


def remote(src, dst, send_sem, recv_sem, device):
    return pltpu.make_async_remote_copy(
        src_ref=src, dst_ref=dst, send_sem=send_sem, recv_sem=recv_sem,
        device_id=device, device_id_type=MESH,
    )


def slot_matrix(ids, tall_too=False):
    wide = jnp.broadcast_to(ids.astype(F32), (TOK, TOK))
    tall = wide.T
    begin = jnp.sum((tall < wide).astype(F32), axis=0, keepdims=True)
    place = lax.broadcasted_iota(jnp.int32, (1, TOK), 1).astype(F32)
    slot = ids.astype(F32) * CAP + place - begin
    slot_wide = jnp.broadcast_to(slot, (SLOTS, TOK))
    onehot = slot_wide == lax.broadcasted_iota(jnp.int32, (SLOTS, TOK), 0).astype(F32)
    onehot = onehot.astype(F32).astype(BF16)
    if not tall_too:
        return onehot
    slot_tall = jnp.broadcast_to(slot, (TOK, TOK)).T
    slot_tall = jnp.concatenate([slot_tall] * (SLOTS // TOK), axis=1)
    flipped = slot_tall == lax.broadcasted_iota(jnp.int32, (TOK, SLOTS), 1).astype(F32)
    return onehot, flipped.astype(F32).astype(BF16)


class RingGather:
    def __init__(self, part, me, device, send, recv, base=0):
        self.part, self.me, self.device = part, me, device
        self.send, self.recv, self.base = send, recv, base

    def copy(self, i):
        place, half, way = (
            (0, 0, 1), (0, 1, 1), (0, 1, -1), (0, 0, -1), (-1, 0, 1), (1, 1, -1)
        )[i]
        part = self.part((self.me + place) % 4, half)
        return remote(
            part, part, self.send.at[self.base + i], self.recv.at[self.base + i], self.device(way)
        )

    def start(self):
        for i in (0, 2, 1, 3):
            self.copy(i).start()

    def forward(self):
        for i in (0, 2):
            self.copy(i).wait_recv()
            self.copy(4 + i // 2).start()

    def finish(self):
        for i in (1, 3, 4, 5):
            self.copy(i).wait_recv()

    def wait_send(self):
        for i in range(6):
            self.copy(i).wait_send()


class PairRingGather:
    def __init__(self, part, me, low, device, send, recv, base=0):
        self.part, self.me, self.low, self.device = part, me, low, device
        self.send, self.recv, self.base = send, recv, base

    def copy(self, i):
        out = 2 * self.low - 1
        place, half, way = (
            (0, None, out), (out, None, -out), (4 - out, 1 - self.low, out), (2, self.low, -out)
        )[i]
        part = self.part((self.me + place + 4) % 4, half)
        return remote(
            part, part, self.send.at[self.base + i], self.recv.at[self.base + i], self.device(way)
        )

    def step(self, i):
        if i:
            self.copy(i - 1).wait_recv()
        if i < 4:
            self.copy(i).start()

    def wait_send(self):
        for i in range(4):
            self.copy(i).wait_send()


class RingReduce:
    def __init__(self, part, me, device, via, near, send, recv, base=0):
        self.part, self.me, self.device = part, me, device
        self.via, self.near, self.send, self.recv, self.base = via, near, send, recv, base

    def copy(self, i):
        place, half, way = ((2, 0, 1), (2, 1, -1), (1, 1, 1), (-1, 0, -1), (1, 0, 1), (-1, 1, -1))[i]
        to = self.via.at[half] if i < 2 else self.near.at[0 if way == 1 else 1, half]
        return remote(
            self.part((self.me + place) % 4, half), to,
            self.send.at[self.base + i], self.recv.at[self.base + i], self.device(way),
        )

    def forward(self):
        for half, place in ((0, 1), (1, -1)):
            self.copy(half).wait_recv()
            part = self.part((self.me + place) % 4, half)
            part[...] = (part[...].astype(F32) + self.via[half].astype(F32)).astype(BF16)
            self.copy(4 + half).start()

    def finish(self):
        for i in range(2, 6):
            self.copy(i).wait_recv()

    def total(self, half):
        own = self.part(self.me, half)[...].astype(F32)
        return own + self.near[0, half].astype(F32) + self.near[1, half].astype(F32)

    def wait_send(self):
        for i in range(6):
            self.copy(i).wait_send()


def kernel(
    rows_ref, target_ref, q_ref, keys_ref, cot_ref, seg_ref, gain_ref, w_ref,
    out_ref, grad_ref,
    r_all, r_other, w_all, q_buf, c_buf, w_buf, qr, cr, kb, pt_s, pt_r, g_s, g_r, g_own,
    gt, a_via, a_near, b_via, b_near, a2_r, b2_r, a1, b1, s3, r3, fin, v_s, v_r, vb, out_buf, st_ref,
    ft_ref, gw,
    local_sem, row_s, row_r, wx_s, wx_r, wx2_s, wx2_r,
    wz_s, wz_r, wz2_s, wz2_r,
    g_ss, g_rs, p_ss, p_rs, go_s, go_r, v_ss, v_rs,
    a_ss, a_rs, b_ss, b_rs, a2_ss, a2_rs, b2_ss, b2_rs, z_ss, z_rs, f_ss, f_rs, fs_s, fs_r, out_sem,
):
    p = lax.axis_index("dp")
    f = lax.axis_index("fsdp")
    zl, y, c = p // 8, (p // 2) % 4, p % 2
    x, zh = f // 4, f % 4
    z = zh * 2 + zl
    sgn = 2 * zl - 1

    def at_z(zz, yy, xx):
        zz = lax.rem(zz + 16, 8)
        return (((zz % 2) * 4 + yy) * 2 + c, xx * 4 + zz // 2)

    def at_x(d):
        return (p, ((x + d) % 4) * 4 + zh)

    def at_y(d):
        return ((zl * 4 + (y + d) % 4) * 2 + c, f)

    sibling = ((zl * 4 + y) * 2 + (1 - c), f)

    loads = [
        pltpu.make_async_copy(w_ref.at[pl.ds(c * DC, DC)], w_buf, local_sem.at[0]),
        pltpu.make_async_copy(q_ref, q_buf, local_sem.at[1]),
        pltpu.make_async_copy(cot_ref, c_buf, local_sem.at[2]),
    ]
    for cp in loads:
        cp.start()

    def row_load(i, half):
        col = pl.multiple_of(i * DSH + half * DC, 128)
        to = pl.multiple_of(i * DC, 128)
        return col, to

    def start_rows(i, _):
        col, to = row_load(i, 1 - c)
        pltpu.make_async_copy(
            rows_ref.at[:, pl.ds(col, DC)], r_other.at[:, pl.ds(to, DC)], local_sem.at[3]
        ).start()
        col, to = row_load(i, c)
        pltpu.make_async_copy(
            rows_ref.at[:, pl.ds(col, DC)], r_all.at[pl.ds(0, TOK), pl.ds(to, DC)], local_sem.at[4]
        ).start()
        return 0

    lax.fori_loop(0, N_FSDP, start_rows, 0)

    barrier = pltpu.get_barrier_semaphore()

    def greet(i, _):
        pl.semaphore_signal(barrier, inc=1, device_id=((p + i) % 16, f), device_id_type=MESH)
        return 0

    lax.fori_loop(1, 16, greet, 0)

    def greet_rings(i, _):
        pl.semaphore_signal(barrier, inc=1, device_id=at_x(i), device_id_type=MESH)
        beside = x * 4 + (zh + i) % 4
        pl.semaphore_signal(barrier, inc=1, device_id=(p, beside), device_id_type=MESH)
        other = ((1 - zl) * 4 + y) * 2 + c
        pl.semaphore_signal(barrier, inc=1, device_id=(other, beside), device_id_type=MESH)
        return 0

    lax.fori_loop(1, 4, greet_rings, 0)

    loads[0].wait()
    own_gain = gain_ref[pl.ds(pl.multiple_of(c * DC, 128), DC)].reshape(1, DC)
    eye = lax.broadcasted_iota(jnp.int32, (DC, DC), 0) == lax.broadcasted_iota(jnp.int32, (DC, DC), 1)
    diagonal = jnp.where(eye, jnp.broadcast_to(own_gain.astype(F32), (DC, DC)), 0.0).astype(BF16)
    w_all[x, zh] = dot(diagonal, w_buf[...]).astype(BF16)
    onehot = slot_matrix(seg_ref[...])
    pl.semaphore_wait(barrier, 15 + 9)

    def wx_copy(j, k):
        first, rows = CHUNKS[j]
        part = w_all.at[x, zh, pl.ds(FIRST_X + first, rows)]
        i = j * 3 + k - 1
        return remote(part, part, wx_s.at[i], wx_r.at[i], at_z(z + sgn * k, y, x))

    def x_part(j):
        first, rows = CHUNKS[j]

        def part(xx, half):
            return w_all.at[xx, :, pl.ds(FIRST_X + first + half * (rows // 2), rows // 2)]

        return part

    wx2 = [RingGather(x_part(j), x, at_x, wx2_s, wx2_r, 6 * j) for j in range(len(CHUNKS))]

    rows_z = ROWS_Z // 2

    def zx_part(xx, half):
        return w_all.at[xx, zh, pl.ds(half * rows_z, rows_z)]

    def z_ring_part(j):
        def part(zz, half):
            first, rows = CHUNKS_Z[j]
            if half is None:
                return w_all.at[:, zz, pl.ds(first, rows)]
            first = first + half * (rows // 2)
            return w_all.at[:, zz, pl.ds(pl.multiple_of(first, 16), rows // 2)]

        return part

    wz = RingGather(zx_part, x, at_x, wz_s, wz_r)
    wz2 = [
        PairRingGather(z_ring_part(j), zh, zl, lambda way: at_z(z + way, y, x), wz2_s, wz2_r, 4 * j)
        for j in range(len(CHUNKS_Z))
    ]

    def start_wx(j):
        for k in (3, 2, 1):
            wx_copy(j, k).start()

    def wait_wx(j):
        for k in (1, 2, 3):
            wx_copy(j, k).wait_recv()

    start_wx(0)
    wz.start()
    start_wx(1)

    row_copy = remote(r_other, r_all.at[pl.ds(TOK, TOK)], row_s, row_r, sibling)
    pltpu.make_async_copy(r_other, r_other, local_sem.at[3]).wait()
    row_copy.start()

    keys_pad = dot(onehot, keys_ref[...]).astype(BF16).reshape(N_DP, 2, 16, KVW)
    kb[...] = jnp.zeros_like(kb)
    for g in range(KV_HEADS):
        lanes = slice(g * 128, (g + 1) * 128)
        kb[:, :, g, :, lanes] = keys_pad[:, :, :, lanes]
    loads[1].wait()
    loads[2].wait()
    for g in range(KV_HEADS):
        wide = slice(g * 1024, (g + 1) * 1024)
        lanes = slice(g * 128, (g + 1) * 128)
        q_pad = dot(onehot, q_buf[:, wide]).astype(BF16).reshape(N_DP, 2, 16, 1024)
        c_pad = dot(onehot, c_buf[:, wide]).astype(BF16).reshape(N_DP, 2, 16, 1024)
        for s in range(GROUP):
            part = slice(s * 128, (s + 1) * 128)
            qr[:, :, s, :, lanes] = q_pad[:, :, :, part]
            cr[:, :, s, :, lanes] = c_pad[:, :, :, part]

    row_i = lax.broadcasted_iota(jnp.int32, (128, 256), 0)
    col_i = lax.broadcasted_iota(jnp.int32, (128, 256), 1)
    allowed = (row_i // 64) * 16 + row_i % 16 <= (col_i // 128) * 16 + col_i % 16

    def g_copy(o):
        return remote(g_s.at[o], g_r.at[p], g_ss.at[o], g_rs.at[p], (o, f))

    def p_copy(o):
        return remote(pt_s.at[o], pt_r.at[p], p_ss.at[o], p_rs.at[p], (o, f))

    def trainer(owners):
        scores = [
            lax.dot_general(
                kb[o].reshape(128, KVW), qr[o].reshape(256, KVW), NT, preferred_element_type=F32
            )
            for o in owners
        ]
        probs = []
        for o, score in zip(owners, scores):
            score = jnp.where(allowed, score * (1.0 / math.sqrt(HEAD_DIM)), -1e30)
            score = score.reshape(2, 4, 16, 256)
            highest = jnp.max(jnp.max(score, axis=0, keepdims=True), axis=2, keepdims=True)
            powers = jnp.exp(score - highest)
            total = jnp.sum(jnp.sum(powers, axis=0, keepdims=True), axis=2, keepdims=True)
            probs.append((powers / total).astype(BF16).reshape(128, 256))
        for o, prob in zip(owners, probs):
            grad = dot(prob, cr[o].reshape(256, KVW)).astype(BF16)
            for kh in range(2):
                for g in range(KV_HEADS):
                    lanes = slice(g * 128, (g + 1) * 128)
                    g_s[o, kh * 16:(kh + 1) * 16, lanes] = (
                        grad[kh * 64 + g * 16:kh * 64 + (g + 1) * 16, lanes]
                    )
            pt_s[o, 0:64] = prob[0:64, 0:128]
            pt_s[o, 64:192] = prob[:, 128:256]

    def trainer_step(i, _):
        owners = [(p + 1 + i * TRAIN + j) % 16 for j in range(TRAIN)]
        trainer(owners)
        for o in owners[:-1]:
            g_copy(o).start()

        @pl.when(i == 0)
        def _():
            g_copy(owners[-1]).start()

        return 0

    lax.fori_loop(0, 16 // TRAIN, trainer_step, 0)

    g_r[p] = g_s[p]
    pt_r[p] = pt_s[p]

    wait_wx(0)
    wx2[0].start()
    wz.forward()

    pltpu.make_async_copy(r_other, r_other, local_sem.at[4]).wait()

    def square(i, acc):
        col = pl.ds(pl.multiple_of(i * 512, 128), 512)
        own = r_all[0:TOK, col].astype(F32)
        oth = r_other[:, col].astype(F32)
        both = own * own + oth * oth
        return acc + both[:, 0:128] + both[:, 128:256] + both[:, 256:384] + both[:, 384:512]

    squares = lax.fori_loop(0, DH // 512, square, jnp.zeros((TOK, 128), F32))
    inverse = lax.rsqrt(jnp.sum(squares, axis=1, keepdims=True) * (1.0 / D) + EPS)
    owner_hot, owner_tall = slot_matrix(target_ref[...], True)
    st_ref[...] = owner_hot
    ft_ref[...] = owner_tall

    def start_p(i, _):
        p_copy((p + i) % 16).start()
        return 0

    lax.fori_loop(1, 16, start_p, 0)

    wz.finish()
    wz2[0].step(0)
    wait_wx(1)
    wx2[1].start()
    wz2[1].step(0)
    wx2[0].forward()

    def wait_g(i, _):
        o = (p + i) % 16
        remote(g_s.at[o], g_r.at[o], g_ss.at[o], g_rs.at[o], (o, f)).wait_recv()
        return 0

    lax.fori_loop(1, 16, wait_g, 0)

    owner_grad = dot(owner_tall, g_r[...].reshape(SLOTS, KVW))
    g_own[0:TOK] = (owner_grad * inverse).astype(BF16)
    go_copy = remote(g_own.at[pl.ds(0, TOK)], g_own.at[pl.ds(TOK, TOK)], go_s, go_r, sibling)
    go_copy.start()

    row_copy.wait()
    go_copy.wait()

    def a_part(q):
        def part(xx, half):
            return gt.at[
                pl.ds(q * PART_A + half * (PART_A // 2), PART_A // 2),
                pl.ds(pl.multiple_of(xx * 1024, 128), 1024),
            ]

        return part

    def b_part(q):
        def part(yy, half):
            return gt.at[
                pl.ds(pl.multiple_of(256 + yy * 64 + q * PART_B, 16), PART_B), pl.ds(half * 2048, 2048)
            ]

        return part

    ring_a = [
        RingReduce(a_part(q), x, at_x, a_via.at[q], a_near.at[q], a_ss, a_rs, 6 * q) for q in range(PARTS)
    ]
    ring_b = [
        RingReduce(b_part(q), y, at_y, b_via.at[q], b_near.at[q], b_ss, b_rs, 6 * q) for q in range(PARTS)
    ]
    gw[...] = g_own[...].T

    def partial(d):
        col = pl.ds(pl.multiple_of(((x + d) % 4) * 1024, 128), 1024)
        gt[:, col] = dot(gw[...], r_all[:, col]).astype(BF16)

    def begin(q):
        for i in range(4):
            ring_a[q].copy(i).start()
        for i in range(4):
            ring_b[q].copy(i).start()

    partial(2)
    ring_a[0].copy(0).start()
    ring_a[0].copy(1).start()
    partial(1)
    ring_a[0].copy(2).start()
    partial(3)
    ring_a[0].copy(3).start()
    partial(0)
    for i in range(4):
        ring_b[0].copy(i).start()
    for q in range(1, PARTS):
        begin(q)

    wx2[1].forward()

    wz2[0].step(1)
    wz2[1].step(1)

    ring_a[0].forward()
    ring_b[0].forward()

    wz2[0].step(2)

    ring_a[1].forward()
    ring_b[1].forward()

    wz2[0].step(3)
    wz2[1].step(2)

    def a2_copy(q, d):
        part = a1.at[q, pl.ds(pl.multiple_of(((y + d) % 4) * PART_B, 16), PART_B)]
        i = q * 3 + d - 1
        return remote(part, a2_r.at[q, d - 1], a2_ss.at[i], a2_rs.at[i], at_y(d))

    def b2_copy(q, d):
        part = b1.at[q, :, pl.ds(pl.multiple_of(((x + d) % 4) * 1024, 128), 1024)]
        i = q * 3 + d - 1
        return remote(part, b2_r.at[q, d - 1], b2_ss.at[i], b2_rs.at[i], at_x(d))

    def second(q):
        ring_a[q].finish()
        for half in range(2):
            rows = slice(half * (PART_A // 2), (half + 1) * (PART_A // 2))
            a1[q, rows] = ring_a[q].total(half).astype(BF16)
        for d in (2, 1, 3):
            a2_copy(q, d).start()
        ring_b[q].finish()
        for half in range(2):
            b1[q, :, half * 2048:(half + 1) * 2048] = ring_b[q].total(half).astype(BF16)
        for d in (2, 1, 3):
            b2_copy(q, d).start()

    second(0)

    wz2[1].step(3)

    second(1)

    own_a = pl.ds(pl.multiple_of(y * PART_B, 16), PART_B)
    own_cols = pl.ds(pl.multiple_of(x * 1024, 128), 1024)

    def z_part(q, zz):
        zz = lax.rem(zz, 8)
        return s3.at[q, :, :, pl.ds(pl.multiple_of(zz * 128, 128), 128)]

    def z_copy(q, k):
        i = q * 7 + k - 1
        return remote(z_part(q, z + k), r3.at[q, k - 1], z_ss.at[i], z_rs.at[i], at_z(z + k, y, x))

    def third(q):
        for d in (1, 2, 3):
            a2_copy(q, d).wait_recv()
        total = a1[q, own_a].astype(F32)
        for d in range(3):
            total = total + a2_r[q, d].astype(F32)
        s3[q, 0] = total.astype(BF16)
        for d in (1, 2, 3):
            b2_copy(q, d).wait_recv()
        total = b1[q, :, own_cols].astype(F32)
        for d in range(3):
            total = total + b2_r[q, d].astype(F32)
        s3[q, 1] = total.astype(BF16)
        for k in (4, 3, 5, 2, 6, 1, 7):
            z_copy(q, k).start()

    for q in range(PARTS // 2):
        third(q)

    for ring in wx2:
        ring.finish()
    for ring in wz2:
        ring.step(4)


    for n in range(2):
        cols = slice(n * 256, (n + 1) * 256)
        v_s[:, cols] = dot(r_all[...], w_all[:, :, :, cols].reshape(DH, 256))
    v_copy = remote(v_s.at[pl.ds(TOK, TOK)], v_r, v_ss, v_rs, sibling)
    v_copy.start()

    for q in range(PARTS // 2, PARTS):
        third(q)

    def f_copy(q, i):
        j = q * 7 + i - 1
        part = fin.at[q, c, p // 2]
        to = (p + i) % 16 if q == PARTS - 1 else (p // 2 + i) % 8 * 2 + c
        return remote(part, part, f_ss.at[j], f_rs.at[j], (to, f))

    def f_peers(q):
        return range(1, 16 if q == PARTS - 1 else 8)

    def fs_copy(q):
        part = fin.at[q, c]
        return remote(part, part, fs_s.at[q], fs_r.at[q], sibling)

    wide_gain = own_gain.astype(F32)
    last_gain = jnp.where(zl == 0, wide_gain[:, :HALF], wide_gain[:, HALF:]).reshape(1, 1, HALF)

    def last(q):
        for k in range(1, 8):
            z_copy(q, k).wait_recv()
        total = z_part(q, z)[...].astype(F32)
        for k in range(7):
            total = total + r3[q, k].astype(F32)
        fin[q, c, p // 2] = (total * last_gain).astype(BF16)
        for i in f_peers(q):
            f_copy(q, i).start()

    for q in range(PARTS // 2):
        last(q)

    v_copy.wait()
    values = ((v_s[0:TOK] + v_r[...]) * inverse).astype(BF16)
    values_pad = dot(st_ref[...], values).astype(BF16).reshape(N_DP, 2, 16, KVW)
    vb[...] = jnp.zeros_like(vb)
    for g in range(KV_HEADS):
        lanes = slice(g * 128, (g + 1) * 128)
        vb[:, :, g, :, lanes] = values_pad[:, :, :, lanes]

    def wait_p(i, _):
        o = (p + i) % 16
        remote(pt_s.at[o], pt_r.at[o], p_ss.at[o], p_rs.at[o], (o, f)).wait_recv()
        return 0

    lax.fori_loop(1, 16, wait_p, 0)

    for q in range(PARTS // 2, PARTS):
        last(q)

    def attend(i, _):
        for t in range(4):
            t = 4 * i + t
            v_t = vb[t].reshape(128, KVW)
            low = lax.dot_general(pt_r[t, 0:64], v_t[0:64], TN, preferred_element_type=F32).astype(BF16)
            high = lax.dot_general(pt_r[t, 64:192], v_t, TN, preferred_element_type=F32).astype(BF16)
            qr[t, 0] = low.reshape(GROUP, 16, KVW)
            qr[t, 1] = high.reshape(GROUP, 16, KVW)
        return 0

    lax.fori_loop(0, N_DP // 4, attend, 0)

    out_copies = []
    for g in range(KV_HEADS):
        lanes = slice(g * 128, (g + 1) * 128)
        wide = slice(g * 1024, (g + 1) * 1024)
        heads = [qr[:, :, s, :, lanes].reshape(SLOTS, 128) for s in range(GROUP)]
        out_buf[:, wide] = dot(ft_ref[...], jnp.concatenate(heads, axis=1)).astype(BF16)
        out_copies.append(
            pltpu.make_async_copy(out_buf.at[:, wide], out_ref.at[:, wide], out_sem.at[g])
        )
        out_copies[-1].start()

    for q in range(PARTS - 1):
        for i in f_peers(q):
            f_copy(q, i).wait_recv()
        fs_copy(q).start()
    for i in f_peers(PARTS - 1):
        f_copy(PARTS - 1, i).wait_recv()
    for q in range(PARTS - 1):
        fs_copy(q).wait_recv()

    for core in range(2):
        for zz in range(2):
            for portion in range(2):
                pieces = []
                for i in range(4 * PARTS):
                    q, yy = (i // 4, i % 4) if portion == 0 else (i % PARTS, i // PARTS)
                    pieces.append(fin[q, core, zz * 4 + yy, portion].astype(F32))
                tall = jnp.concatenate(pieces, axis=0)
                first = core * DC + zz * HALF
                grad_ref[first:first + HALF, portion * 256:(portion + 1) * 256] = tall.T

    for cp in out_copies:
        cp.wait()
    for ring in wx2 + [wz] + wz2 + ring_a + ring_b:
        ring.wait_send()
    for k in (1, 2, 3):
        for j in range(len(CHUNKS)):
            wx_copy(j, k).wait_send()
        for q in range(PARTS):
            a2_copy(q, k).wait_send()
            b2_copy(q, k).wait_send()
    for k in range(1, 8):
        for q in range(PARTS):
            z_copy(q, k).wait_send()
    for q in range(PARTS):
        for i in f_peers(q):
            f_copy(q, i).wait_send()
    for q in range(PARTS - 1):
        fs_copy(q).wait_send()

    def wait_sends(i, _):
        g_copy((p + i) % 16).wait_send()
        p_copy((p + i) % 16).wait_send()
        return 0

    lax.fori_loop(1, 16, wait_sends, 0)


def results(returned_ref, gradient_ref, out_ref, grad_ref, out_buf, grad_buf, in_sem, out_sem):
    arrive, leave = [], []
    for i in range(6):
        if i < 4:
            rows = pl.ds(i * (TOK // 4), TOK // 4)
            refs = returned_ref.at[rows], out_buf.at[rows], out_ref.at[rows]
        else:
            rows = pl.ds((i - 4) * (DSH // 2), DSH // 2)
            refs = gradient_ref.at[rows], grad_buf.at[rows], grad_ref.at[rows]
        arrive.append(pltpu.make_async_copy(refs[0], refs[1], in_sem.at[i]))
        leave.append(pltpu.make_async_copy(refs[1], refs[2], out_sem.at[i]))
    for cp in arrive:
        cp.start()
    for first, second in zip(arrive, leave):
        first.wait()
        second.start()
    for cp in leave:
        cp.wait()


def on_device(rows_owned, target, offset, queries, keys, cotangent, segment, norm_gain, value_weight):
    dma = pltpu.SemaphoreType.DMA
    vmem = pltpu.VMEM
    scratch = [
        vmem((2 * TOK, DH), BF16),
        vmem((TOK, DH), BF16),
        vmem((4, 4, DC, KVW), BF16),
        vmem((TOK, QW), BF16),
        vmem((TOK, QW), BF16),
        vmem((DC, KVW), BF16),
        vmem((N_DP, 2, GROUP, 16, KVW), BF16),
        vmem((N_DP, 2, GROUP, 16, KVW), BF16),
        vmem((N_DP, 2, KV_HEADS, 16, KVW), BF16),
        vmem((N_DP, 192, 128), BF16),
        vmem((N_DP, 192, 128), BF16),
        vmem((N_DP, CAP, KVW), BF16),
        vmem((N_DP, CAP, KVW), BF16),
        vmem((2 * TOK, KVW), BF16),
        vmem((KVW, DH), BF16),
        vmem((PARTS, 2, PART_A // 2, 1024), BF16),
        vmem((PARTS, 2, 2, PART_A // 2, 1024), BF16),
        vmem((PARTS, 2, PART_B, 2048), BF16),
        vmem((PARTS, 2, 2, PART_B, 2048), BF16),
        vmem((PARTS, 3, PART_B, 1024), BF16),
        vmem((PARTS, 3, PART_B, 1024), BF16),
        vmem((PARTS, PART_A, 1024), BF16),
        vmem((PARTS, PART_B, DH), BF16),
        vmem((PARTS, 2, PART_B, 1024), BF16),
        vmem((PARTS, 7, 2, PART_B, HALF), BF16),
        vmem((PARTS, 2, 8, 2, PART_B, HALF), BF16),
        vmem((2 * TOK, KVW), F32),
        vmem((TOK, KVW), F32),
        vmem((N_DP, 2, KV_HEADS, 16, KVW), BF16),
        vmem((TOK, QW), BF16),
        vmem((SLOTS, TOK), BF16),
        vmem((TOK, SLOTS), BF16),
        vmem((KVW, 2 * TOK), BF16),
        dma((5,)),
        dma, dma,
        dma((3 * len(CHUNKS),)), dma((3 * len(CHUNKS),)),
        dma((6 * len(CHUNKS),)), dma((6 * len(CHUNKS),)),
        dma((6,)), dma((6,)), dma((4 * len(CHUNKS_Z),)), dma((4 * len(CHUNKS_Z),)),
        dma((16,)), dma((16,)), dma((16,)), dma((16,)),
        dma, dma, dma, dma,
        dma((24,)), dma((24,)), dma((24,)), dma((24,)),
        dma((12,)), dma((12,)), dma((12,)), dma((12,)),
        dma((28,)), dma((28,)), dma((36,)), dma((36,)), dma((3,)), dma((3,)),
        dma((KV_HEADS,)),
    ]
    anywhere = pl.BlockSpec(memory_space=pl.ANY)
    inside = pl.BlockSpec(memory_space=pltpu.VMEM)
    returned, gradient = pl.pallas_call(
        kernel,
        out_shape=(
            jax.ShapeDtypeStruct((TOK, QW), BF16),
            jax.ShapeDtypeStruct((DSH, KVW), F32),
        ),
        in_specs=[anywhere, inside, anywhere, inside, anywhere, inside, inside, anywhere],
        out_specs=(anywhere, inside),
        scratch_shapes=scratch,
        compiler_params=pltpu.CompilerParams(
            collective_id=0, has_side_effects=True, vmem_limit_bytes=60 * 2**20
        ),
        cost_estimate=pl.CostEstimate(flops=8 * 10**9, bytes_accessed=16 * 2**20, transcendentals=10**6),
        name="value_path",
    )(
        rows_owned.reshape(TOK, D),
        target.reshape(1, TOK),
        queries.reshape(TOK, QW),
        keys.reshape(TOK, KVW),
        cotangent.reshape(TOK, QW),
        segment.reshape(1, TOK),
        norm_gain,
        value_weight,
    )
    returned, gradient = pl.pallas_call(
        results,
        out_shape=(
            jax.ShapeDtypeStruct((TOK, QW), BF16),
            jax.ShapeDtypeStruct((DSH, KVW), F32),
        ),
        in_specs=[anywhere, anywhere],
        out_specs=(anywhere, anywhere),
        scratch_shapes=[vmem((TOK, QW), BF16), vmem((DSH, KVW), F32), dma((6,)), dma((6,))],
        name="results",
    )(returned, gradient)
    return (returned.reshape(1, 1, TOK, QW), gradient)


def solution(mesh):
    placed = (
        P("dp", "fsdp", None, None),
        P("dp", "fsdp", None),
        P("dp", "fsdp", None),
        P("dp", "fsdp", None, None),
        P("dp", "fsdp", None, None),
        P("dp", "fsdp", None, None),
        P("dp", "fsdp", None),
        P("fsdp"),
        P("fsdp", None),
    )
    return jax.shard_map(
        on_device,
        mesh=mesh,
        in_specs=placed,
        out_specs=(P("dp", "fsdp", None, None), P("fsdp", None)),
        check_vma=False,
    )
```
